256 devices in a mesh: grp: 8 (over z_lo, core), dev: 32 (over x, y, z_hi).
Axes of the slice: x: 4, y: 4, z: 8 (z_hi: 2, z_lo: 4; z = z_hi * 4 + z_lo), core: 2. Of those that a mesh axis runs over, the one named last changes fastest.
Arguments:
- query_raw: bfloat16 [16384, 1024], P(('grp', 'dev')), may hold values from -6 to 6
- key_raw: bfloat16 [16384, 128], P(('grp', 'dev')), may hold values from -6 to 6
- resp_values: bfloat16 [16384, 128], P(('grp', 'dev')), may hold values from -6 to 6
- attn_out: bfloat16 [16384, 1024], P(('grp', 'dev')), may hold values from -3 to 3
- out_grad: bfloat16 [16384, 1024], P(('grp', 'dev')), may hold values from -6 to 6
- prompt_keys: bfloat16 [65536, 128], P(('grp', 'dev')), may hold values from -2 to 2
- prompt_values: bfloat16 [65536, 128], P(('grp', 'dev')), may hold values from -6 to 6
- query_gain: float32 [128], replicated, may hold values from 0.5 to 1.5
- key_gain: float32 [128], replicated, may hold values from 1.5 to 4
- resp_lengths: int32 [8, 64], P('grp'), may hold values from 1 to 63, as said below
- resp_holder: int32 [8, 64], P('grp'), may hold values from 0 to 31, as said below
Outputs:
- query_raw_grad: bfloat16 [16384, 1024], P(('grp', 'dev'))
- key_raw_grad: bfloat16 [16384, 128], P(('grp', 'dev'))
- resp_value_grad: bfloat16 [16384, 128], P(('grp', 'dev'))
- prompt_key_grad: float32 [65536, 128], P(('grp', 'dev'))
- prompt_value_grad: float32 [65536, 128], P(('grp', 'dev'))
- query_gain_grad: float32 [128], replicated
- key_gain_grad: float32 [128], replicated
The draws below stay inside these ranges and needn't reach their ends.
Inputs may be any that keep to these rules, and one draw needn't show every extreme that they name: `resp_holder`: every device of a group holds exactly 2 responses. `resp_lengths`: the responses held by one device have lengths summing to at most 64; in each group at least one device holds responses whose lengths sum to exactly 64; the others may hold fewer.
All inputs are finite; a program needn't handle non-finite values.
Results may differ from the reference program's by a relative error of at most 0.03.
Values may be sent and summed in bfloat16 or wider, within the bound.
A program may use at most 64 MiB of HBM per device.

```python
import math
import jax
import jax.numpy as jnp
from jax import lax

HD = 128
CAP = 64
RESP_DEV = 2
GROUPS = 8
PLEN = 8192
NRESP = 64
QW = 1024
ROWS = 16384
PROWS = 65536
N_DEV = 32


def shared_layout(key):

    def per_group(group_key):
        key_order, key_shift, key_fullest, key_split = jax.random.split(group_key, 4)
        devices = NRESP // RESP_DEV
        ranking = jax.random.permutation(key_order, NRESP).astype(jnp.int32)
        holder = ranking // RESP_DEV
        within = ranking % RESP_DEV
        shifts = jax.random.randint(key_shift, (devices,), 0, 4)
        fullest = jax.random.randint(key_fullest, (), 0, devices)
        is_fullest = jnp.arange(devices) == fullest
        shifts = jnp.where(is_fullest, 0, shifts)
        totals = CAP // jnp.left_shift(jnp.int32(1), shifts)
        divide = jax.random.randint(key_split, (devices,), 1, totals)
        divide = jnp.where(is_fullest, 1, divide)
        opening = divide[holder]
        amount = totals[holder]
        lengths = jnp.where(within == 0, opening, amount - opening)
        return (lengths.astype(jnp.int32), holder.astype(jnp.int32))
    return jax.vmap(per_group)(jax.random.split(key, GROUPS))


def draw_resp_lengths(key, part):
    layout = shared_layout(key)
    return layout[0]


def draw_resp_holder(key, part):
    layout = shared_layout(key)
    return layout[1]


def levels(rng, extent, cuts, low, top_value):
    factor_of = 1.0
    for dim, blocks in cuts:
        steps = jax.random.uniform(jax.random.fold_in(jax.random.fold_in(rng, 6), dim), (blocks,), jnp.float32, low / len(cuts), top_value / len(cuts))
        factor_of = factor_of * jnp.repeat(jnp.exp(steps), extent[dim] // blocks).reshape((-1,) + (1,) * (len(extent) - 1 - dim))
    return factor_of


def centred(key, extent, width, limit, cuts=(), kind=jnp.bfloat16):
    values = width * jax.random.normal(key, extent, jnp.float32)
    if cuts:
        values = values * levels(key, extent, cuts, -0.22, 0.18)
    return jnp.clip(values, -limit, limit).astype(kind)


def setup_inputs(seed: int = 0) -> dict:
    splits = jax.random.split(jax.random.key(seed), 12)
    query_raw = centred(splits[0], (ROWS, QW), 1.0, 6.0, ((0, 256),))
    key_raw = centred(splits[1], (ROWS, HD), 1.0, 6.0, ((0, 256),))
    resp_values = centred(splits[2], (ROWS, HD), 1.0, 6.0, ((0, 256),))
    attn_out = centred(splits[3], (ROWS, QW), 0.5, 3.0, ((0, 256),))
    out_grad = centred(splits[4], (ROWS, QW), 1.0, 6.0, ((0, 256),))
    prompt_keys = centred(splits[5], (PROWS, HD), 0.5, 2.0, ((0, 256),))
    prompt_values = centred(splits[6], (PROWS, HD), 1.0, 6.0, ((0, 256),))
    query_gain = jnp.clip(1.0 + 0.1 * jax.random.normal(splits[7], (HD,), jnp.float32), 0.5, 1.5)
    key_gain = jnp.clip(jnp.exp(jax.random.uniform(splits[8], (HD,), jnp.float32, math.log(1.5), math.log(4.0))), 1.5, 4.0)
    resp_lengths = draw_resp_lengths(jax.random.fold_in(splits[11], 71), 0)
    resp_holder = draw_resp_holder(jax.random.fold_in(splits[11], 71), 0)
    return dict(query_raw=query_raw, key_raw=key_raw, resp_values=resp_values, attn_out=attn_out, out_grad=out_grad, prompt_keys=prompt_keys, prompt_values=prompt_values, query_gain=query_gain, key_gain=key_gain, resp_lengths=resp_lengths, resp_holder=resp_holder)


norm_eps = 1e-06

def layout_rows(lengths, holders, device_idx, slots):
    own_len = jnp.where(holders == device_idx, lengths, 0)
    seg_ends = jnp.cumsum(own_len, dtype=jnp.int32)
    row_ids = jnp.arange(slots, dtype=jnp.int32)
    segment = lax.optimization_barrier(jnp.sum((seg_ends[None, :] <= row_ids[:, None]).astype(jnp.int32), axis=1, dtype=jnp.int32))
    is_valid = row_ids < seg_ends[-1]
    allowed = (segment[:, None] == segment[None, :]) & (row_ids[None, :] <= row_ids[:, None])
    allowed = allowed & is_valid[:, None] & is_valid[None, :]
    return (is_valid, allowed)

def rms_forward(raw, gains):
    widened = raw.astype(jnp.float32)
    inverse = lax.rsqrt(lax.optimization_barrier(jnp.mean(widened * widened, axis=-1, keepdims=True)) + norm_eps)
    return (widened, inverse, widened * inverse * gains)

def rms_backward(widened, inverse, gains, upstream):
    scaled = upstream * gains
    raw_grad = inverse * scaled - widened * inverse ** 3 * lax.optimization_barrier(jnp.mean(scaled * widened, axis=-1, keepdims=True))
    gain_grad = lax.optimization_barrier(jnp.sum((upstream * widened * inverse).reshape(-1, widened.shape[-1]), axis=0))
    return (raw_grad, gain_grad)

def local_terms(query_raw, key_raw, attn_out, out_grad, query_gain, key_gain, allowed):
    slots, head_dim = key_raw.shape
    head_num = query_raw.shape[1] // head_dim
    query_wide, query_inverse, query_normed = rms_forward(query_raw.reshape(slots, head_num, head_dim), query_gain)
    key_wide, key_inverse, key_normed = rms_forward(key_raw, key_gain)
    queries = query_normed.astype(jnp.bfloat16).reshape(slots * head_num, head_dim)
    own_keys = key_normed.astype(jnp.bfloat16)
    grad_rows = out_grad.reshape(slots * head_num, head_dim)
    products = (out_grad.astype(jnp.float32) * attn_out.astype(jnp.float32)).reshape(slots * head_num, head_dim)
    out_dot = lax.optimization_barrier(jnp.sum(products, axis=1))
    score_scale = head_dim ** (-0.5)
    self_scores = jnp.dot(queries, own_keys.T, preferred_element_type=jnp.float32) * score_scale
    self_exp = jnp.where(jnp.repeat(allowed, head_num, axis=0), jnp.exp(self_scores), jnp.zeros_like(self_scores))
    return (query_wide, query_inverse, key_wide, key_inverse, queries, own_keys, grad_rows, out_dot, self_exp)

def self_grads(self_exp, norm_total, out_dot, queries, own_keys, grad_rows, resp_values, score_scale):
    attn_prob = self_exp / norm_total[:, None]
    prob_low = attn_prob.astype(jnp.bfloat16)
    prob_grad = jnp.dot(grad_rows, resp_values.T, preferred_element_type=jnp.float32)
    score_grad = (attn_prob * (prob_grad - out_dot[:, None])).astype(jnp.bfloat16)
    query_part = jnp.dot(score_grad, own_keys, preferred_element_type=jnp.float32)
    key_grad = jnp.dot(score_grad.T, queries, preferred_element_type=jnp.float32) * score_scale
    value_grad = jnp.dot(prob_low.T, grad_rows, preferred_element_type=jnp.float32)
    return (query_part, key_grad, value_grad)

def prompt_totals(queries, keys, score_scale, block_len):

    def advance(running, key_block):
        scores = jnp.dot(queries, key_block.T, preferred_element_type=jnp.float32) * score_scale
        return (running + lax.optimization_barrier(jnp.sum(jnp.exp(scores), axis=1)), None)
    start = jnp.zeros((queries.shape[0],), jnp.float32)
    running, unused = lax.scan(advance, start, keys.reshape(-1, block_len, keys.shape[1]))
    return running

def prompt_grads(queries, grad_rows, keys, values, norm_total, out_dot, row_live, score_scale, block_len):
    head_dim = keys.shape[1]

    def advance(running, blocks):
        key_block, val_block = blocks
        scores = jnp.dot(queries, key_block.T, preferred_element_type=jnp.float32) * score_scale
        attn_prob = jnp.exp(scores) / norm_total[:, None] * row_live[:, None]
        prob_low = attn_prob.astype(jnp.bfloat16)
        prob_grad = jnp.dot(grad_rows, val_block.T, preferred_element_type=jnp.float32)
        score_grad = (attn_prob * (prob_grad - out_dot[:, None])).astype(jnp.bfloat16)
        running = running + jnp.dot(score_grad, key_block, preferred_element_type=jnp.float32)
        key_part = jnp.dot(score_grad.T, queries, preferred_element_type=jnp.float32) * score_scale
        value_part = jnp.dot(prob_low.T, grad_rows, preferred_element_type=jnp.float32)
        return (running, (key_part, value_part))
    start = jnp.zeros((queries.shape[0], head_dim), jnp.float32)
    blocks = (keys.reshape(-1, block_len, head_dim), values.reshape(-1, block_len, head_dim))
    running, (key_grad, value_grad) = lax.scan(advance, start, blocks)
    return (running, key_grad.reshape(-1, head_dim), value_grad.reshape(-1, head_dim))

def device_grads(query_raw, key_raw, resp_values, attn_out, out_grad, keys, values, query_gain, key_gain, lengths, holders, device_idx):
    slots, head_dim = key_raw.shape
    head_num = query_raw.shape[1] // head_dim
    score_scale = head_dim ** (-0.5)
    block_len = min(2048, keys.shape[0])
    is_valid, allowed = layout_rows(lengths, holders, device_idx, slots)
    terms = local_terms(query_raw, key_raw, attn_out, out_grad, query_gain, key_gain, allowed)
    query_wide, query_inverse, key_wide, key_inverse, queries, own_keys, grad_rows, out_dot, self_exp = terms
    norm_total = prompt_totals(queries, keys, score_scale, block_len) + lax.optimization_barrier(jnp.sum(self_exp, axis=1))
    row_live = jnp.repeat(is_valid, head_num).astype(jnp.float32)
    prompt_query, key_grad, value_grad = prompt_grads(queries, grad_rows, keys, values, norm_total, out_dot, row_live, score_scale, block_len)
    self_query, self_key, self_value = self_grads(self_exp, norm_total, out_dot, queries, own_keys, grad_rows, resp_values, score_scale)
    query_norm_grad = (score_scale * (prompt_query + self_query)).reshape(slots, head_num, head_dim)
    query_raw_grad, query_gain_part = rms_backward(query_wide, query_inverse, query_gain, query_norm_grad)
    key_raw_grad, key_gain_part = rms_backward(key_wide, key_inverse, key_gain, self_key)
    return (query_raw_grad.reshape(slots, head_num * head_dim).astype(jnp.bfloat16), key_raw_grad.astype(jnp.bfloat16), self_value.astype(jnp.bfloat16), key_grad, value_grad, query_gain_part, key_gain_part)

def reference(query_raw, key_raw, resp_values, attn_out, out_grad, prompt_keys, prompt_values, query_gain, key_gain, resp_lengths, resp_holder):

    def per_device(array):
        return array.reshape(GROUPS, N_DEV, CAP, array.shape[-1])

    def group_pass(group_in):
        query_g, key_g, value_g, output_g, grad_g, keys_g, values_g, lengths, holders = group_in

        def device_pass(running, device_in):
            query_d, key_d, value_d, output_d, grad_d, device_idx = device_in
            results = device_grads(query_d, key_d, value_d, output_d, grad_d, keys_g, values_g, query_gain, key_gain, lengths, holders, device_idx)
            running = (running[0] + results[3], running[1] + results[4], running[2] + results[5], running[3] + results[6])
            return (running, (results[0], results[1], results[2]))
        start = (jnp.zeros((PLEN, HD), jnp.float32), jnp.zeros((PLEN, HD), jnp.float32), jnp.zeros((HD,), jnp.float32), jnp.zeros((HD,), jnp.float32))
        device_ids = jnp.arange(N_DEV, dtype=jnp.int32)
        return lax.scan(device_pass, start, (query_g, key_g, value_g, output_g, grad_g, device_ids))
    inputs = (per_device(query_raw), per_device(key_raw), per_device(resp_values), per_device(attn_out), per_device(out_grad), prompt_keys.reshape(GROUPS, PLEN, HD), prompt_values.reshape(GROUPS, PLEN, HD), resp_lengths, resp_holder)
    sums, rows_out = lax.map(group_pass, inputs)
    return (rows_out[0].reshape(ROWS, QW), rows_out[1].reshape(ROWS, HD), rows_out[2].reshape(ROWS, HD), sums[0].reshape(PROWS, HD), sums[1].reshape(PROWS, HD), lax.optimization_barrier(jnp.sum(sums[2], axis=0)), lax.optimization_barrier(jnp.sum(sums[3], axis=0)))
```

```python
import functools
import math

import jax
import jax.numpy as jnp
from jax import lax
from jax.experimental import pallas as pl
from jax.experimental.pallas import tpu as pltpu
from jax.sharding import PartitionSpec as P

f32 = jnp.float32
bf16 = jnp.bfloat16
MESH = pl.DeviceIdType.MESH
EPS = 1e-06
HEADS = 8
HD = 128
CAP = 64
ROWS = HEADS * CAP
KEYS = 256
NT = (((1,), (1,)), ((), ()))
NN = (((1,), (0,)), ((), ()))
TN = (((0,), (0,)), ((), ()))
S_Q, S_D, S_K, S_N, S_G, S_R, S_Z, S_X, S_Y, S_V, S_C = 0, 4, 8, 16, 20, 24, 40, 42, 46, 50, 58
N_SEM = 60


def dot(a, b, dims):
    return lax.dot_general(a, b, dims, preferred_element_type=f32)


def kernel(
    qr_ref, kr_ref, rv_ref, ao_ref, og_ref, pk_ref, pv_ref, qg_ref, kg_ref, len_ref, hold_ref,
    oq_ref, ok_ref, ov_ref, opk_ref, opv_ref, oqg_ref, okg_ref,
    qb, db, kb, kt, eg, dqt, rs, rss, rsr, qn, invr, dqs, dqsend, dqr,
    se, sg, sb, acc, rr, zs, zr, gx, gy, gz, gc, gsrc, send, recv,
):
    grp = lax.axis_index("grp")
    dev = lax.axis_index("dev")
    x, y, z = dev // 8, (dev // 2) % 4, (dev % 2) * 4 + grp // 2
    core = grp % 2
    scale = HD ** (-0.5)

    def at(x=x, y=y, z=z, core=core):
        return ((z % 4) * 2 + core, x * 8 + y * 2 + z // 4)

    def xk(k):
        return at(x=(x + 4 - k) % 4)

    def yk(k):
        return at(y=(y + 4 - k) % 4)

    def zk(k):
        return at(z=(z + 8 - k) % 8)

    def copy(src, dst, sem, to):
        return pltpu.make_async_remote_copy(
            src_ref=src, dst_ref=dst, send_sem=send.at[sem], recv_sem=recv.at[sem],
            device_id=to, device_id_type=MESH,
        )

    def q_copy(k):
        return copy(qb.at[0], qb.at[k], S_Q + k, xk(k))

    def d_copy(k):
        return copy(db.at[0], db.at[k], S_D + k, xk(k))

    def k_copy(j):
        if j == 4:
            return copy(kb.at[0], kb.at[4], S_K + 4, zk(4))
        return copy(kb.at[j // 4 * 4], kb.at[j], S_K + j, yk(j % 4))

    def n_copy(k):
        return copy(rss, rsr.at[k], S_N + k, xk(k))

    def g_copy(k):
        return copy(dqsend.at[4 - k], dqr.at[k], S_G + k, xk(k))

    def r_copy(plane, t, kk):
        s = (4 - kk) % 4
        return copy(
            sb.at[plane, t, kk], rr.at[plane, t, s], S_R + plane * 8 + t * 4 + s, yk(s)
        )

    def z_copy(t):
        return copy(zs.at[t], zr.at[t], S_Z + t, zk(4))

    def gx_copy(k):
        return copy(gsrc.at[0], gx.at[x], S_X + k, xk(k))

    def gy_copy(k):
        return copy(gsrc.at[1], gy.at[y], S_Y + k, yk(k))

    def gz_copy(k):
        return copy(gsrc.at[2], gz.at[z], S_V + k, zk(k))

    def gc_copy():
        return copy(gsrc.at[3], gc.at[core], S_C, at(core=1 - core))

    barrier = pltpu.get_barrier_semaphore()
    partners = [xk(k) for k in (1, 2, 3)] + [yk(k) for k in (1, 2, 3)]
    partners += [zk(k) for k in range(1, 8)] + [at(core=1 - core)]
    for to in partners:
        pl.semaphore_signal(barrier, inc=1, device_id=to, device_id_type=MESH)

    kb[0, 0] = pk_ref[...]
    kb[0, 1] = pv_ref[...]
    held = hold_ref[...] == dev
    mine = jnp.where(held, len_ref[...].astype(f32), 0.0)
    place = lax.broadcasted_iota(jnp.int32, (1, 64), 1).astype(f32)
    total = jnp.sum(mine, axis=1, keepdims=True)
    first = jnp.min(jnp.where(held, place, 64.0), axis=1, keepdims=True)
    len1 = jnp.sum(jnp.where(place == first, mine, 0.0), axis=1, keepdims=True)
    live = lax.broadcasted_iota(jnp.int32, (CAP, HD), 0).astype(f32) < total
    gain = qg_ref[...]

    def q_head(h):
        wide = qr_ref[:, h * HD : (h + 1) * HD].astype(f32)
        inv = lax.rsqrt(jnp.mean(wide * wide, axis=1, keepdims=True) + EPS)
        return wide, inv

    ones = jnp.ones((8, HD), bf16)
    for h in range(HEADS):
        cols = slice(h * HD, (h + 1) * HD)
        rows = slice(h * CAP, (h + 1) * CAP)
        wide, inv = q_head(h)
        normed = wide * inv * (gain * (scale * math.log2(math.e)))
        qb[0, 0, rows, :] = jnp.where(live, normed, 0.0).astype(bf16)
        grad = jnp.where(live, og_ref[:, cols].astype(f32), 0.0)
        qb[0, 1, rows, :] = grad.astype(bf16)
        prod = grad * ao_ref[:, cols].astype(f32)
        high = prod.astype(bf16)
        low = (prod - high.astype(f32)).astype(bf16)
        sb[0, 0, h // 4, (h % 4) * CAP : (h % 4 + 1) * CAP, :] = high
        sb[0, 1, h // 4, (h % 4) * CAP : (h % 4 + 1) * CAP, :] = low
    for half in range(2):
        lanes = slice(half * KEYS, (half + 1) * KEYS)
        db[0, :, lanes] = dot(ones, sb[0, 0, half], NT) + dot(ones, sb[0, 1, half], NT)

    pl.semaphore_wait(barrier, len(partners))
    k_copy(4).start()
    for j in (2, 1, 3):
        k_copy(j).start()
    for k in (1, 3, 2):
        q_copy(k).start()
        d_copy(k).start()

    key_wide = kr_ref[...].astype(f32)
    key_inv = lax.rsqrt(jnp.mean(key_wide * key_wide, axis=1, keepdims=True) + EPS)
    own_keys = (key_wide * key_inv * kg_ref[...]).astype(bf16)
    slot_j = lax.broadcasted_iota(jnp.int32, (CAP, ROWS), 0)
    slot_i = lax.broadcasted_iota(jnp.int32, (CAP, ROWS), 1) & (CAP - 1)
    slot_j, slot_i = slot_j.astype(f32), slot_i.astype(f32)
    seg_j = jnp.where(slot_j >= len1, 1.0, 0.0)
    seg_i = jnp.where(slot_i >= len1, 1.0, 0.0)
    allowed = (slot_j <= slot_i) & (slot_i < total) & (seg_j == seg_i)
    e = jnp.where(allowed, jnp.exp2(dot(own_keys, qb[0, 0], NT)), 0.0)
    g = e * (dot(rv_ref[...], qb[0, 1], NT) - db[0, 0:1, :])
    rs[0] = jnp.sum(e.reshape(CAP // 8, 8, ROWS), axis=0)
    for i in range(1, 4):
        rs[i] = jnp.zeros((8, ROWS), f32)
    se[...] = e.astype(bf16)
    sg[...] = g.astype(bf16)
    dqs[...] = dot(own_keys, sg[...], TN)

    def block(keys, values, i):
        n = keys.shape[0]
        e = jnp.exp2(dot(keys, qb[i, 0], NT)).reshape(n // 8, 8, ROWS)
        rs[i] += jnp.sum(e, axis=0)
        p = dot(values, qb[i, 1], NT).reshape(n // 8, 8, ROWS)
        g = e * (p - db[i][None])
        return e.reshape(n, ROWS).astype(bf16), g.reshape(n, ROWS).astype(bf16)

    kt[:, 0:KEYS] = kb[0, 0].T
    for j in (1, 3, 2):
        k_copy(j).wait_recv()
        kt[:, j * KEYS : (j + 1) * KEYS] = kb[j, 0].T

    def near(m, carry):
        i = jnp.where(m == 2, 3, jnp.where(m == 3, 2, m))

        for k, step in ((1, 1), (3, 2), (2, 3)):

            @pl.when(m == step)
            def _():
                q_copy(k).wait_recv()
                d_copy(k).wait_recv()

        @pl.when(m == 2)
        def _():
            k_copy(4).wait_recv()
            for j in (6, 5, 7):
                k_copy(j).start()

        e, g = block(
            kb[0:4, 0].reshape(4 * KEYS, HD), kb[0:4, 1].reshape(4 * KEYS, HD), i
        )
        eg[0, 0:4, i] = e.reshape(4, KEYS, ROWS)
        eg[1, 0:4, i] = g.reshape(4, KEYS, ROWS)
        dqt[i] = dot(kt[...], g, NN)
        return carry

    lax.fori_loop(0, 4, near, 0)

    def far(m, carry):
        j = jnp.where(m == 2, 7, jnp.where(m == 3, 6, m + 4))

        for jj, step in ((5, 1), (7, 2), (6, 3)):

            @pl.when(m == step)
            def _():
                k_copy(jj).wait_recv()

        keys, values = kb[j, 0], kb[j, 1]
        turned = keys.T
        for i in range(4):
            e, g = block(keys, values, i)
            eg[0, j, i] = e
            eg[1, j, i] = g
            dqt[i] += dot(turned, g, NN)
        return carry

    lax.fori_loop(0, 4, far, 0)

    rss[...] = jnp.zeros((8, ROWS), f32)
    for i in range(4):
        rss[i : i + 1, :] = jnp.sum(rs[i], axis=0, keepdims=True)
    for k in (2, 1, 3):
        n_copy(k).start()
    for i in (2, 1, 3):
        dqsend[i] = dqt[i].astype(bf16)
        g_copy(4 - i).start()
    for k in (1, 3, 2):
        n_copy(k).wait_recv()
    for i in range(4):
        norm = rss[i : i + 1, :]
        for k in (1, 2, 3):
            r = (i + 4 - k) % 4
            norm = norm + rsr[k, r : r + 1, :]
        inv = 1.0 / norm
        if i == 0:
            invr[...] = jnp.broadcast_to(inv, (8, ROWS))
        for c in range(4):
            part = slice(c * HD, (c + 1) * HD)
            column = jnp.broadcast_to(inv[:, part], (HD, HD)).T
            qn[0, i, part, :] = (qb[i, 1, part, :].astype(f32) * column).astype(bf16)
            column = column * math.log(2.0)
            qn[1, i, part, :] = (qb[i, 0, part, :].astype(f32) * column).astype(bf16)

    def plane_sum(plane, t):
        for s in (1, 3, 2):
            r_copy(plane, t, 4 - s).wait_recv()
        total = acc[plane, t]
        for s in (1, 2, 3):
            total = total + rr[plane, t, s].astype(f32)
        return total

    def to_plane(t):
        zs[t] = plane_sum(1, t).astype(bf16)
        z_copy(t).start()

    def terms(n, carry):
        plane = 1 - n // 8
        t = (n // 4) % 2
        m = n % 4
        kk = jnp.where(m == 0, 2, jnp.where(m == 2, 3, jnp.where(m == 3, 0, 1)))

        @pl.when(n == 12)
        def _():
            to_plane(0)

        j = plane * 4 + kk
        part = dot(eg[t, j, 0], qn[t, 0], NN)
        for i in range(1, 4):
            part = part + dot(eg[t, j, i], qn[t, i], NN)
        sb[plane, t, kk] = part.astype(bf16)

        @pl.when(m < 3)
        def _():
            r_copy(plane, t, kk).start()

        @pl.when(m == 3)
        def _():
            acc[plane, t] = part

        return carry

    lax.fori_loop(0, 16, terms, 0)
    to_plane(1)

    ov_ref[...] = dot(se[...], qn[0, 0], NN).astype(bf16)
    kng = dot(sg[...], qn[1, 0], NN)
    w = kng * kg_ref[...]
    mean = jnp.mean(w * key_wide, axis=1, keepdims=True)
    ok_ref[...] = (key_inv * w - key_wide * (key_inv * key_inv * key_inv * mean)).astype(bf16)
    key_gain = jnp.sum(kng * key_wide * key_inv, axis=0, keepdims=True)

    for k in (1, 3, 2):
        g_copy(k).wait_recv()
    query_gain = jnp.zeros((1, HD), f32)
    for c in range(4):
        part = slice(c * HD, (c + 1) * HD)
        turned = dqt[0, :, part] + dqs[:, part]
        for k in (1, 2, 3):
            turned = turned + dqr[k, :, part].astype(f32)
        grad = (turned * (invr[0:1, part] * scale)).T
        for h in (2 * c, 2 * c + 1):
            qng = grad[(h % 2) * CAP : (h % 2 + 1) * CAP, :]
            wide, inv = q_head(h)
            u = qng * gain
            mean = jnp.mean(u * wide, axis=1, keepdims=True)
            oq_ref[:, h * HD : (h + 1) * HD] = (inv * u - wide * (inv * inv * inv * mean)).astype(bf16)
            query_gain = query_gain + jnp.sum(qng * wide * inv, axis=0, keepdims=True)

    both = jnp.concatenate([query_gain, key_gain, jnp.zeros((6, HD), f32)], axis=0)
    gsrc[0] = both
    gx[x] = both
    for k in (2, 1, 3):
        gx_copy(k).start()

    near_sum = [plane_sum(0, 0), plane_sum(0, 1)]

    for k in (1, 3, 2):
        gx_copy(k).wait_recv()
    both = gx[0] + gx[1] + gx[2] + gx[3]
    gsrc[1] = both
    gy[y] = both
    for k in (2, 1, 3):
        gy_copy(k).start()
    opv_ref[...] = near_sum[0]
    opk_ref[...] = near_sum[1]
    for k in (1, 3, 2):
        gy_copy(k).wait_recv()
    both = gy[0] + gy[1] + gy[2] + gy[3]
    gsrc[2] = both
    gz[z] = both
    for k in (4, 3, 5, 2, 6, 1, 7):
        gz_copy(k).start()
    z_copy(0).wait_recv()
    opv_ref[...] += zr[0].astype(f32)
    z_copy(1).wait_recv()
    opk_ref[...] += zr[1].astype(f32)
    for k in range(1, 8):
        gz_copy(k).wait_recv()
    both = gz[0]
    for k in range(1, 8):
        both = both + gz[k]
    gsrc[3] = both
    gc[core] = both
    gc_copy().start()
    gc_copy().wait_recv()
    both = gc[0] + gc[1]
    oqg_ref[...] = both[0:1, :]
    okg_ref[...] = both[1:2, :]

    for j in range(1, 8):
        k_copy(j).wait_send()
    for k in (1, 2, 3):
        for make in (q_copy, d_copy, n_copy, g_copy, gx_copy, gy_copy):
            make(k).wait_send()
        for plane in range(2):
            for t in range(2):
                r_copy(plane, t, k).wait_send()
    for t in range(2):
        z_copy(t).wait_send()
    for k in range(1, 8):
        gz_copy(k).wait_send()
    gc_copy().wait_send()


def shards(qr, kr, rv, ao, og, pk, pv, qg, kg, lengths, holders):
    vmem = pl.BlockSpec(memory_space=pltpu.VMEM)
    outs = pl.pallas_call(
        kernel,
        name="attention_backward",
        out_shape=(
            jax.ShapeDtypeStruct((CAP, HEADS * HD), bf16),
            jax.ShapeDtypeStruct((CAP, HD), bf16),
            jax.ShapeDtypeStruct((CAP, HD), bf16),
            jax.ShapeDtypeStruct((KEYS, HD), f32),
            jax.ShapeDtypeStruct((KEYS, HD), f32),
            jax.ShapeDtypeStruct((1, HD), f32),
            jax.ShapeDtypeStruct((1, HD), f32),
        ),
        in_specs=[vmem] * 11,
        out_specs=(vmem,) * 7,
        scratch_shapes=[
            pltpu.VMEM((4, 2, ROWS, HD), bf16),
            pltpu.VMEM((4, 8, ROWS), f32),
            pltpu.VMEM((8, 2, KEYS, HD), bf16),
            pltpu.VMEM((HD, 4 * KEYS), bf16),
            pltpu.VMEM((2, 8, 4, KEYS, ROWS), bf16),
            pltpu.VMEM((4, HD, ROWS), f32),
            pltpu.VMEM((4, 8, ROWS), f32),
            pltpu.VMEM((8, ROWS), f32),
            pltpu.VMEM((4, 8, ROWS), f32),
            pltpu.VMEM((2, 4, ROWS, HD), bf16),
            pltpu.VMEM((8, ROWS), f32),
            pltpu.VMEM((HD, ROWS), f32),
            pltpu.VMEM((4, HD, ROWS), bf16),
            pltpu.VMEM((4, HD, ROWS), bf16),
            pltpu.VMEM((CAP, ROWS), bf16),
            pltpu.VMEM((CAP, ROWS), bf16),
            pltpu.VMEM((2, 2, 4, KEYS, HD), bf16),
            pltpu.VMEM((2, 2, KEYS, HD), f32),
            pltpu.VMEM((2, 2, 4, KEYS, HD), bf16),
            pltpu.VMEM((2, KEYS, HD), bf16),
            pltpu.VMEM((2, KEYS, HD), bf16),
            pltpu.VMEM((4, 8, HD), f32),
            pltpu.VMEM((4, 8, HD), f32),
            pltpu.VMEM((8, 8, HD), f32),
            pltpu.VMEM((2, 8, HD), f32),
            pltpu.VMEM((4, 8, HD), f32),
            pltpu.SemaphoreType.DMA((N_SEM,)),
            pltpu.SemaphoreType.DMA((N_SEM,)),
        ],
        compiler_params=pltpu.CompilerParams(
            collective_id=0, has_side_effects=True, vmem_limit_bytes=52 << 20
        ),
    )(qr, kr, rv, ao, og, pk, pv, qg.reshape(1, HD), kg.reshape(1, HD), lengths, holders)
    return (*outs[:5], outs[5].reshape(HD), outs[6].reshape(HD))


def solution(mesh):
    rows = P(("grp", "dev"), None)
    return jax.shard_map(
        shards,
        mesh=mesh,
        in_specs=(rows,) * 7 + (P(), P(), P("grp", None), P("grp", None)),
        out_specs=(rows,) * 5 + (P(), P()),
        check_vma=False,
    )
```

```python
import functools
import math

import jax
import jax.numpy as jnp
from jax import lax
from jax.experimental import pallas as pl
from jax.experimental.pallas import tpu as pltpu
from jax.sharding import PartitionSpec as P

f32 = jnp.float32
bf16 = jnp.bfloat16
MESH = pl.DeviceIdType.MESH
EPS = 1e-06
HEADS = 8
HD = 128
CAP = 64
ROWS = HEADS * CAP
KEYS = 256
NT = (((1,), (1,)), ((), ()))
NN = (((1,), (0,)), ((), ()))
TN = (((0,), (0,)), ((), ()))
S_Q, S_D, S_K, S_N, S_G, S_R, S_Z, S_X, S_Y, S_V, S_C = 0, 8, 12, 28, 32, 36, 52, 54, 58, 62, 70
N_SEM = 71


def dot(a, b, dims):
    return lax.dot_general(a, b, dims, preferred_element_type=f32)


def kernel(
    qr_in, kr_in, rv_in, ao_in, og_in, pk_in, pv_in, qg_in, kg_in, len_in, hold_in,
    oq_out, ok_out, ov_out, opk_out, opv_out, oqg_out, okg_out,
    oq_ref, ok_ref, ov_ref, opk_ref, opv_ref, oqg_ref, okg_ref,
    qr_ref, kr_ref, rv_ref, ao_ref, og_ref, qg_ref, kg_ref, len_ref, hold_ref,
    qb, db, kb, kt, eg, dqt, rs, rss, rsr, qn, invr, dqs, dqsend, dqr,
    se, sg, sb, acc, rr, zs, zr, gx, gy, gz, gc, gsrc, send, recv, load, store,
):
    grp = lax.axis_index("grp")
    dev = lax.axis_index("dev")
    x, y, z = dev // 8, (dev // 2) % 4, (dev % 2) * 4 + grp // 2
    core = grp % 2
    scale = HD ** (-0.5)

    def at(x=x, y=y, z=z, core=core):
        return ((z % 4) * 2 + core, x * 8 + y * 2 + z // 4)

    def xk(k):
        return at(x=(x + 4 - k) % 4)

    def yk(k):
        return at(y=(y + 4 - k) % 4)

    def zk(k):
        return at(z=(z + 8 - k) % 8)

    def copy(src, dst, sem, to):
        return pltpu.make_async_remote_copy(
            src_ref=src, dst_ref=dst, send_sem=send.at[sem], recv_sem=recv.at[sem],
            device_id=to, device_id_type=MESH,
        )

    def q_copy(k, p):
        src = qb.at[0, p] if k != 2 else qb.at[3 - 2 * p, p]
        return copy(src, qb.at[k, p], S_Q + 2 * k + p, xk(k if k != 2 else 3 - 2 * p))

    def d_copy(k):
        return copy(db.at[0], db.at[k], S_D + k, xk(k))

    def k_copy(j, p):
        src = (pk_in, pv_in)[p] if j <= 4 else kb.at[4, p]
        return copy(src, kb.at[j, p], S_K + 2 * j + p, zk(4) if j == 4 else yk(j % 4))

    def n_copy(k):
        return copy(rss, rsr.at[k], S_N + k, xk(k))

    def g_copy(k):
        return copy(dqsend.at[4 - k], dqr.at[k], S_G + k, xk(k))

    def r_copy(plane, t, kk):
        s = (4 - kk) % 4
        return copy(
            sb.at[plane, t, kk], rr.at[plane, t, s], S_R + plane * 8 + t * 4 + s, yk(s)
        )

    def z_copy(t):
        return copy(zs.at[t], zr.at[t], S_Z + t, zk(4))

    def gx_copy(k):
        return copy(gsrc.at[0], gx.at[x], S_X + k, xk(k))

    def gy_copy(k):
        return copy(gsrc.at[1], gy.at[y], S_Y + k, yk(k))

    def gz_copy(k):
        return copy(gsrc.at[2], gz.at[z], S_V + k, zk(k))

    def gc_copy():
        return copy(gsrc.at[3], gc.at[core], S_C, at(core=1 - core))

    loads = [
        pltpu.make_async_copy(src, dst, load.at[n])
        for n, (src, dst) in enumerate(
            (
                (pk_in, kb.at[0, 0]), (pv_in, kb.at[0, 1]), (hold_in, hold_ref), (len_in, len_ref),
                (qg_in, qg_ref), (kg_in, kg_ref), (qr_in, qr_ref), (og_in, og_ref), (ao_in, ao_ref),
                (kr_in, kr_ref), (rv_in, rv_ref),
            )
        )
    ]
    for one in loads:
        one.start()

    stores = [
        pltpu.make_async_copy(src, dst, store.at[n])
        for n, (src, dst) in enumerate(
            (
                (oq_ref, oq_out), (ok_ref, ok_out), (ov_ref, ov_out), (opk_ref, opk_out),
                (opv_ref, opv_out), (oqg_ref, oqg_out), (okg_ref, okg_out),
            )
        )
    ]

    barrier = pltpu.get_barrier_semaphore()
    partners = [xk(k) for k in (1, 2, 3)] + [yk(k) for k in (1, 2, 3)]
    partners += [zk(k) for k in range(1, 8)] + [at(core=1 - core)]
    for to in partners:
        pl.semaphore_signal(barrier, inc=1, device_id=to, device_id_type=MESH)

    pl.semaphore_wait(barrier, len(partners))
    for p in range(2):
        k_copy(4, p).start()
    for p in range(2):
        for j in (1, 3, 2):
            k_copy(j, p).start()
    for one in loads:
        one.wait()
    held = hold_ref[...] == dev
    mine = jnp.where(held, len_ref[...].astype(f32), 0.0)
    place = lax.broadcasted_iota(jnp.int32, (1, 64), 1).astype(f32)
    total = jnp.sum(mine, axis=1, keepdims=True)
    first = jnp.min(jnp.where(held, place, 64.0), axis=1, keepdims=True)
    len1 = jnp.sum(jnp.where(place == first, mine, 0.0), axis=1, keepdims=True)
    live = lax.broadcasted_iota(jnp.int32, (CAP, HD), 0).astype(f32) < total
    gain = qg_ref[...]

    def q_head(h):
        wide = qr_ref[:, h * HD : (h + 1) * HD].astype(f32)
        inv = lax.rsqrt(jnp.mean(wide * wide, axis=1, keepdims=True) + EPS)
        return wide, inv

    ones = jnp.ones((8, HD), bf16)
    for h in range(HEADS):
        cols = slice(h * HD, (h + 1) * HD)
        rows = slice(h * CAP, (h + 1) * CAP)
        wide, inv = q_head(h)
        normed = wide * inv * (gain * (scale * math.log2(math.e)))
        qb[0, 0, rows, :] = jnp.where(live, normed, 0.0).astype(bf16)
        grad = jnp.where(live, og_ref[:, cols].astype(f32), 0.0)
        qb[0, 1, rows, :] = grad.astype(bf16)
        prod = grad * ao_ref[:, cols].astype(f32)
        high = prod.astype(bf16)
        low = (prod - high.astype(f32)).astype(bf16)
        sb[0, 0, h // 4, (h % 4) * CAP : (h % 4 + 1) * CAP, :] = high
        sb[0, 1, h // 4, (h % 4) * CAP : (h % 4 + 1) * CAP, :] = low
    for half in range(2):
        lanes = slice(half * KEYS, (half + 1) * KEYS)
        both = dot(ones, sb[0, 0, half], NT) + dot(ones, sb[0, 1, half], NT)
        db[0, :, lanes] = both[0:1, :]

    for p in range(2):
        q_copy(3, p).start()
        q_copy(1, 1 - p).start()
    for k in (1, 3, 2):
        d_copy(k).start()

    key_wide = kr_ref[...].astype(f32)
    key_inv = lax.rsqrt(jnp.mean(key_wide * key_wide, axis=1, keepdims=True) + EPS)
    own_keys = (key_wide * key_inv * kg_ref[...]).astype(bf16)
    slot_j = lax.broadcasted_iota(jnp.int32, (CAP, ROWS), 0)
    slot_i = lax.broadcasted_iota(jnp.int32, (CAP, ROWS), 1) & (CAP - 1)
    slot_j, slot_i = slot_j.astype(f32), slot_i.astype(f32)
    seg_j = jnp.where(slot_j >= len1, 1.0, 0.0)
    seg_i = jnp.where(slot_i >= len1, 1.0, 0.0)
    allowed = (slot_j <= slot_i) & (slot_i < total) & (seg_j == seg_i)
    e = jnp.where(allowed, jnp.exp2(dot(own_keys, qb[0, 0], NT)), 0.0)
    g = e * (dot(rv_ref[...], qb[0, 1], NT) - db[0])
    rs[0] = jnp.sum(e.reshape(CAP // 8, 8, ROWS), axis=0)
    for i in range(1, 4):
        rs[i] = jnp.zeros((8, ROWS), f32)
    se[...] = e.astype(bf16)
    sg[...] = g.astype(bf16)
    dqs[...] = dot(own_keys, sg[...], TN)

    def block(keys, values, i):
        n = keys.shape[0]
        e = jnp.exp2(dot(keys, qb[i, 0], NT))
        rs[i] += jnp.sum(e.reshape(n // 8, 8, ROWS), axis=0)
        g = e * (dot(values, qb[i, 1], NT) - db[i])
        return e.astype(bf16), g.astype(bf16)

    q_copy(3, 0).wait_recv()
    q_copy(2, 0).start()
    q_copy(1, 1).wait_recv()
    q_copy(2, 1).start()
    kt[0, :, 0:KEYS] = kb[0, 0].T
    for j in (1, 3, 2):
        k_copy(j, 0).wait_recv()
        kt[0, :, j * KEYS : (j + 1) * KEYS] = kb[j, 0].T
    for j in (1, 3, 2):
        k_copy(j, 1).wait_recv()

    def pass_on(p):
        k_copy(4, p).wait_recv()
        for j in (5, 7, 6):
            k_copy(j, p).start()

    pass_on(0)

    def near(m, carry):
        i = jnp.where(m == 2, 3, jnp.where(m == 3, 2, m))

        @pl.when(m == 1)
        def _():
            pass_on(1)
            q_copy(1, 0).wait_recv()
            d_copy(1).wait_recv()

        @pl.when(m == 2)
        def _():
            q_copy(3, 1).wait_recv()
            d_copy(3).wait_recv()

        @pl.when(m == 3)
        def _():
            q_copy(2, 0).wait_recv()
            q_copy(2, 1).wait_recv()
            d_copy(2).wait_recv()

        e, g = block(
            kb[0:4, 0].reshape(4 * KEYS, HD), kb[0:4, 1].reshape(4 * KEYS, HD), i
        )
        eg[0, 0:4, i] = e.reshape(4, KEYS, ROWS)
        eg[1, 0:4, i] = g.reshape(4, KEYS, ROWS)
        dqt[i] = dot(kt[0], g, NN)
        return carry

    lax.fori_loop(0, 4, near, 0)

    def far(m, carry):
        j = jnp.where(m == 2, 7, jnp.where(m == 3, 6, m + 4))

        for jj, step in ((5, 1), (7, 2), (6, 3)):

            @pl.when(m == step)
            def _():
                k_copy(jj, 0).wait_recv()
                k_copy(jj, 1).wait_recv()

        keys, values = kb[j, 0], kb[j, 1]
        for i in range(4):
            e, g = block(keys, values, i)
            eg[0, j, i] = e
            eg[1, j, i] = g
        return carry

    lax.fori_loop(0, 4, far, 0)

    for i in range(4):
        rss[i] = jnp.sum(rs[i], axis=0, keepdims=True)
    for k in (2, 1, 3):
        n_copy(k).start()

    for j in range(4):
        kt[1, :, j * KEYS : (j + 1) * KEYS] = kb[4 + j, 0].T

    def rest(m, carry):
        i = (m + 2) % 4
        dqt[i] += dot(kt[1], eg[1, 4:8, i].reshape(4 * KEYS, ROWS), NN)
        dqsend[i] = dqt[i].astype(bf16)

        for k in (1, 2, 3):

            @pl.when(i == 4 - k)
            def _():
                g_copy(k).start()

        return carry

    lax.fori_loop(0, 4, rest, 0)
    dqt[0] += dqs[...]
    dqsend[0] = dqt[0].astype(bf16)
    for k in (1, 3, 2):
        n_copy(k).wait_recv()
    for i in range(4):
        norm = rss[i]
        for k in (1, 2, 3):
            norm = norm + rsr[k, (i + 4 - k) % 4]
        inv = 1.0 / norm
        if i == 0:
            invr[...] = inv
        for c in range(4):
            part = slice(c * HD, (c + 1) * HD)
            column = jnp.broadcast_to(inv[:, part], (HD, HD)).T
            qn[0, i, part, :] = (qb[i, 1, part, :].astype(f32) * column).astype(bf16)
            column = column * math.log(2.0)
            qn[1, i, part, :] = (qb[i, 0, part, :].astype(f32) * column).astype(bf16)

    def plane_sum(plane, t):
        for s in (1, 3, 2):
            r_copy(plane, t, 4 - s).wait_recv()
        total = acc[plane, t]
        for s in (1, 2, 3):
            total = total + rr[plane, t, s].astype(f32)
        return total

    def to_plane(t):
        zs[t] = plane_sum(1, t).astype(bf16)
        z_copy(t).start()

    def own_terms():
        ov_ref[...] = dot(se[...], qn[0, 0], NN).astype(bf16)
        kng = dot(sg[...], qn[1, 0], NN)
        wide = kr_ref[...].astype(f32)
        inv = lax.rsqrt(jnp.mean(wide * wide, axis=1, keepdims=True) + EPS)
        w = kng * kg_ref[...]
        mean = jnp.mean(w * wide, axis=1, keepdims=True)
        ok_ref[...] = (inv * w - wide * (inv * inv * inv * mean)).astype(bf16)
        stores[1].start()
        stores[2].start()
        key_gain = jnp.sum(kng * wide * inv, axis=0, keepdims=True)
        square = dot(dqsend[0], qn[1, 0], NN)
        for i in range(1, 4):
            square = square + dot(dqsend[i], qn[1, i], NN)
        one = lax.broadcasted_iota(jnp.int32, (HD, HD), 0)
        two = lax.broadcasted_iota(jnp.int32, (HD, HD), 1)
        query_gain = jnp.sum(jnp.where(one == two, square, 0.0), axis=0, keepdims=True) / gain
        both = jnp.concatenate([query_gain, key_gain, jnp.zeros((6, HD), f32)], axis=0)
        gsrc[0] = both
        gx[x] = both
        for k in (2, 1, 3):
            gx_copy(k).start()

    def gains_y():
        for k in (1, 3, 2):
            gx_copy(k).wait_recv()
        both = gx[0] + gx[1] + gx[2] + gx[3]
        gsrc[1] = both
        gy[y] = both
        for k in (2, 1, 3):
            gy_copy(k).start()

    def gains_z():
        for k in (1, 3, 2):
            gy_copy(k).wait_recv()
        both = gy[0] + gy[1] + gy[2] + gy[3]
        gsrc[2] = both
        gz[z] = both
        for k in (4, 3, 5, 2, 6, 1, 7):
            gz_copy(k).start()

    def gains_core():
        for k in range(1, 8):
            gz_copy(k).wait_recv()
        both = gz[0]
        for k in range(1, 8):
            both = both + gz[k]
        gsrc[3] = both
        gc[core] = both
        gc_copy().start()

    def terms(n, carry):
        plane = 1 - n // 8
        t = (n // 4) % 2
        m = n % 4
        kk = jnp.where(m == 0, 2, jnp.where(m == 2, 3, jnp.where(m == 3, 0, 1)))

        @pl.when(n == 4)
        def _():
            own_terms()

        @pl.when(n == 8)
        def _():
            gains_y()

        @pl.when(n == 12)
        def _():
            to_plane(0)

        @pl.when(n == 13)
        def _():
            gains_z()

        j = plane * 4 + kk
        part = dot(eg[t, j, 0], qn[t, 0], NN)
        for i in range(1, 4):
            part = part + dot(eg[t, j, i], qn[t, i], NN)
        sb[plane, t, kk] = part.astype(bf16)

        @pl.when(m < 3)
        def _():
            r_copy(plane, t, kk).start()

        @pl.when(m == 3)
        def _():
            acc[plane, t] = part

        return carry

    lax.fori_loop(0, 16, terms, 0)
    to_plane(1)

    for k in (1, 3, 2):
        g_copy(k).wait_recv()
    for c in range(4):
        part = slice(c * HD, (c + 1) * HD)
        turned = dqt[0, :, part]
        for k in (1, 2, 3):
            turned = turned + dqr[k, :, part].astype(f32)
        grad = (turned * (invr[:, part] * scale)).T
        for h in (2 * c, 2 * c + 1):
            wide, inv = q_head(h)
            u = grad[(h % 2) * CAP : (h % 2 + 1) * CAP, :] * gain
            mean = jnp.mean(u * wide, axis=1, keepdims=True)
            found = inv * u - wide * (inv * inv * inv * mean)
            oq_ref[:, h * HD : (h + 1) * HD] = found.astype(bf16)
    stores[0].start()

    opv_ref[...] = plane_sum(0, 0)
    opk_ref[...] = plane_sum(0, 1)
    gains_core()
    z_copy(0).wait_recv()
    opv_ref[...] += zr[0].astype(f32)
    stores[4].start()
    z_copy(1).wait_recv()
    opk_ref[...] += zr[1].astype(f32)
    stores[3].start()
    gc_copy().wait_recv()
    both = gc[0] + gc[1]
    oqg_ref[...] = both[0:1, :]
    okg_ref[...] = both[1:2, :]
    stores[5].start()
    stores[6].start()

    for p in range(2):
        for j in range(1, 8):
            k_copy(j, p).wait_send()
        for k in (1, 2, 3):
            q_copy(k, p).wait_send()
    for k in (1, 2, 3):
        for make in (d_copy, n_copy, g_copy, gx_copy, gy_copy):
            make(k).wait_send()
        for plane in range(2):
            for t in range(2):
                r_copy(plane, t, k).wait_send()
    for t in range(2):
        z_copy(t).wait_send()
    for k in range(1, 8):
        gz_copy(k).wait_send()
    gc_copy().wait_send()
    for one in stores:
        one.wait()


def deliver(*refs):
    into, out = refs[21], refs[22]
    first = [pltpu.make_async_copy(refs[i], refs[14 + i], into.at[i]) for i in range(7)]
    then = [pltpu.make_async_copy(refs[14 + i], refs[7 + i], out.at[i]) for i in range(7)]
    for one in first:
        one.start()
    for one, two in zip(first, then, strict=True):
        one.wait()
        two.start()
    for two in then:
        two.wait()


def shards(qr, kr, rv, ao, og, pk, pv, qg, kg, lengths, holders):
    shapes = (
        jax.ShapeDtypeStruct((CAP, HEADS * HD), bf16),
        jax.ShapeDtypeStruct((CAP, HD), bf16),
        jax.ShapeDtypeStruct((CAP, HD), bf16),
        jax.ShapeDtypeStruct((KEYS, HD), f32),
        jax.ShapeDtypeStruct((KEYS, HD), f32),
        jax.ShapeDtypeStruct((1, HD), f32),
        jax.ShapeDtypeStruct((1, HD), f32),
    )
    somewhere = pl.BlockSpec(memory_space=pl.ANY)
    outs = pl.pallas_call(
        kernel,
        name="attention_backward",
        out_shape=shapes,
        in_specs=[somewhere] * 11,
        out_specs=(somewhere,) * 7,
        scratch_shapes=[
            pltpu.VMEM((CAP, HEADS * HD), bf16),
            pltpu.VMEM((CAP, HD), bf16),
            pltpu.VMEM((CAP, HD), bf16),
            pltpu.VMEM((KEYS, HD), f32),
            pltpu.VMEM((KEYS, HD), f32),
            pltpu.VMEM((1, HD), f32),
            pltpu.VMEM((1, HD), f32),
            pltpu.VMEM((CAP, HEADS * HD), bf16),
            pltpu.VMEM((CAP, HD), bf16),
            pltpu.VMEM((CAP, HD), bf16),
            pltpu.VMEM((CAP, HEADS * HD), bf16),
            pltpu.VMEM((CAP, HEADS * HD), bf16),
            pltpu.VMEM((1, HD), f32),
            pltpu.VMEM((1, HD), f32),
            pltpu.VMEM((1, 64), jnp.int32),
            pltpu.VMEM((1, 64), jnp.int32),
            pltpu.VMEM((4, 2, ROWS, HD), bf16),
            pltpu.VMEM((4, 1, ROWS), f32),
            pltpu.VMEM((8, 2, KEYS, HD), bf16),
            pltpu.VMEM((2, HD, 4 * KEYS), bf16),
            pltpu.VMEM((2, 8, 4, KEYS, ROWS), bf16),
            pltpu.VMEM((4, HD, ROWS), f32),
            pltpu.VMEM((4, 8, ROWS), f32),
            pltpu.VMEM((4, 1, ROWS), f32),
            pltpu.VMEM((4, 4, 1, ROWS), f32),
            pltpu.VMEM((2, 4, ROWS, HD), bf16),
            pltpu.VMEM((1, ROWS), f32),
            pltpu.VMEM((HD, ROWS), f32),
            pltpu.VMEM((4, HD, ROWS), bf16),
            pltpu.VMEM((4, HD, ROWS), bf16),
            pltpu.VMEM((CAP, ROWS), bf16),
            pltpu.VMEM((CAP, ROWS), bf16),
            pltpu.VMEM((2, 2, 4, KEYS, HD), bf16),
            pltpu.VMEM((2, 2, KEYS, HD), f32),
            pltpu.VMEM((2, 2, 4, KEYS, HD), bf16),
            pltpu.VMEM((2, KEYS, HD), bf16),
            pltpu.VMEM((2, KEYS, HD), bf16),
            pltpu.VMEM((4, 8, HD), f32),
            pltpu.VMEM((4, 8, HD), f32),
            pltpu.VMEM((8, 8, HD), f32),
            pltpu.VMEM((2, 8, HD), f32),
            pltpu.VMEM((4, 8, HD), f32),
            pltpu.SemaphoreType.DMA((N_SEM,)),
            pltpu.SemaphoreType.DMA((N_SEM,)),
            pltpu.SemaphoreType.DMA((11,)),
            pltpu.SemaphoreType.DMA((7,)),
        ],
        compiler_params=pltpu.CompilerParams(
            collective_id=0, has_side_effects=True, vmem_limit_bytes=60 << 20
        ),
    )(qr, kr, rv, ao, og, pk, pv, qg.reshape(1, HD), kg.reshape(1, HD), lengths, holders)
    outs = pl.pallas_call(
        deliver,
        name="deliver",
        out_shape=shapes,
        in_specs=[somewhere] * 7,
        out_specs=(somewhere,) * 7,
        scratch_shapes=[pltpu.VMEM(shape.shape, shape.dtype) for shape in shapes]
        + [pltpu.SemaphoreType.DMA((7,))] * 2,
        compiler_params=pltpu.CompilerParams(vmem_limit_bytes=60 << 20),
    )(*outs)
    return (*outs[:5], outs[5].reshape(HD), outs[6].reshape(HD))


def solution(mesh):
    rows = P(("grp", "dev"), None)
    return jax.shard_map(
        shards,
        mesh=mesh,
        in_specs=(rows,) * 7 + (P(), P(), P("grp", None), P("grp", None)),
        out_specs=(rows,) * 5 + (P(), P()),
        check_vma=False,
    )
```

```python
import functools
import math

import jax
import jax.numpy as jnp
from jax import lax
from jax.experimental import pallas as pl
from jax.experimental.pallas import tpu as pltpu
from jax.sharding import PartitionSpec as P

f32 = jnp.float32
bf16 = jnp.bfloat16
MESH = pl.DeviceIdType.MESH
EPS = 1e-06
HEADS = 8
HD = 128
CAP = 64
ROWS = HEADS * CAP
KEYS = 256
NT = (((1,), (1,)), ((), ()))
NN = (((1,), (0,)), ((), ()))
TN = (((0,), (0,)), ((), ()))
S_Q, S_D, S_K, S_N, S_G, S_R, S_Z, S_X, S_Y, S_V = 0, 8, 12, 28, 32, 36, 52, 54, 62, 66
N_SEM = 74


def dot(a, b, dims):
    return lax.dot_general(a, b, dims, preferred_element_type=f32)


def kernel(
    qr_in, kr_in, rv_in, ao_in, og_in, pk_in, pv_in, qg_in, kg_in, len_in, hold_in,
    oq_out, ok_out, ov_out, opk_out, opv_out, zr_out, gx_out,
    oq_ref, ok_ref, ov_ref, opk_ref, opv_ref,
    qr_ref, kr_ref, rv_ref, ao_ref, og_ref, qg_ref, kg_ref, len_ref, hold_ref,
    qb, db, kb, kt, eg, dqt, rs, rss, rsr, qn, invr, dqs, dqsend, dqr,
    se, sg, sb, acc, rr, zs, gy, gz, gsrc, send, recv, load, store,
):
    grp = lax.axis_index("grp")
    dev = lax.axis_index("dev")
    x, y, z = dev // 8, (dev // 2) % 4, (dev % 2) * 4 + grp // 2
    core = grp % 2
    scale = HD ** (-0.5)

    def at(x=x, y=y, z=z, core=core):
        return ((z % 4) * 2 + core, x * 8 + y * 2 + z // 4)

    def xk(k):
        return at(x=(x + 4 - k) % 4)

    def yk(k):
        return at(y=(y + 4 - k) % 4)

    def zk(k):
        return at(z=(z + 8 - k) % 8)

    def copy(src, dst, sem, to):
        return pltpu.make_async_remote_copy(
            src_ref=src, dst_ref=dst, send_sem=send.at[sem], recv_sem=recv.at[sem],
            device_id=to, device_id_type=MESH,
        )

    def q_copy(k, p):
        src = qb.at[0, p] if k != 2 else qb.at[3 - 2 * p, p]
        return copy(src, qb.at[k, p], S_Q + 2 * k + p, xk(k if k != 2 else 3 - 2 * p))

    def d_copy(k):
        return copy(db.at[0], db.at[k], S_D + k, xk(k))

    def k_copy(j, p):
        src = (pk_in, pv_in)[p] if j <= 4 else kb.at[4, p]
        return copy(src, kb.at[j, p], S_K + 2 * j + p, zk(4) if j == 4 else yk(j % 4))

    def n_copy(k):
        return copy(rss, rsr.at[k], S_N + k, xk(k))

    def g_copy(k):
        return copy(dqsend.at[4 - k], dqr.at[k], S_G + k, xk(k))

    def r_copy(plane, t, kk):
        s = (4 - kk) % 4
        return copy(
            sb.at[plane, t, kk], rr.at[plane, t, s], S_R + plane * 8 + t * 4 + s, yk(s)
        )

    def z_copy(t):
        return copy(zs.at[t], zr_out.at[t], S_Z + t, zk(4))

    def gx_to(k):
        return at(x=(x + 4 - k // 2) % 4, core=(core + k) % 2)

    def gz_copy(k):
        return copy(gsrc.at[0], gz.at[z], S_V + k, zk(k))

    def gy_copy(k):
        return copy(gsrc.at[1], gy.at[y], S_Y + k, yk(k))

    def gx_copy(k):
        return copy(gsrc.at[2], gx_out.at[x * 2 + core], S_X + k, gx_to(k))

    loads = [
        pltpu.make_async_copy(src, dst, load.at[n])
        for n, (src, dst) in enumerate(
            (
                (pk_in, kb.at[0, 0]), (pv_in, kb.at[0, 1]), (hold_in, hold_ref), (len_in, len_ref),
                (qg_in, qg_ref), (kg_in, kg_ref), (qr_in, qr_ref), (og_in, og_ref), (ao_in, ao_ref),
                (kr_in, kr_ref), (rv_in, rv_ref),
            )
        )
    ]
    for one in loads:
        one.start()

    stores = [
        pltpu.make_async_copy(src, dst, store.at[n])
        for n, (src, dst) in enumerate(
            (
                (oq_ref, oq_out), (ok_ref, ok_out), (ov_ref, ov_out), (opk_ref, opk_out),
                (opv_ref, opv_out), (gsrc.at[2], gx_out.at[x * 2 + core]),
            )
        )
    ]

    barrier = pltpu.get_barrier_semaphore()
    partners = [gx_to(k) for k in range(1, 8)] + [yk(k) for k in (1, 2, 3)]
    partners += [zk(k) for k in range(1, 8)]
    for to in partners:
        pl.semaphore_signal(barrier, inc=1, device_id=to, device_id_type=MESH)

    pl.semaphore_wait(barrier, len(partners))
    for p in range(2):
        k_copy(4, p).start()
    for p in range(2):
        for j in (1, 3, 2):
            k_copy(j, p).start()
    for one in loads:
        one.wait()
    held = hold_ref[...] == dev
    mine = jnp.where(held, len_ref[...].astype(f32), 0.0)
    place = lax.broadcasted_iota(jnp.int32, (1, 64), 1).astype(f32)
    total = jnp.sum(mine, axis=1, keepdims=True)
    first = jnp.min(jnp.where(held, place, 64.0), axis=1, keepdims=True)
    len1 = jnp.sum(jnp.where(place == first, mine, 0.0), axis=1, keepdims=True)
    live = lax.broadcasted_iota(jnp.int32, (CAP, HD), 0).astype(f32) < total
    gain = qg_ref[...]

    def q_head(h):
        wide = qr_ref[:, h * HD : (h + 1) * HD].astype(f32)
        inv = lax.rsqrt(jnp.mean(wide * wide, axis=1, keepdims=True) + EPS)
        return wide, inv

    ones = jnp.ones((8, HD), bf16)
    for h in range(HEADS):
        cols = slice(h * HD, (h + 1) * HD)
        rows = slice(h * CAP, (h + 1) * CAP)
        wide, inv = q_head(h)
        normed = wide * inv * (gain * (scale * math.log2(math.e)))
        qb[0, 0, rows, :] = jnp.where(live, normed, 0.0).astype(bf16)
        grad = jnp.where(live, og_ref[:, cols].astype(f32), 0.0)
        qb[0, 1, rows, :] = grad.astype(bf16)
        prod = grad * ao_ref[:, cols].astype(f32)
        high = prod.astype(bf16)
        low = (prod - high.astype(f32)).astype(bf16)
        sb[0, 0, h // 4, (h % 4) * CAP : (h % 4 + 1) * CAP, :] = high
        sb[0, 1, h // 4, (h % 4) * CAP : (h % 4 + 1) * CAP, :] = low
    for half in range(2):
        lanes = slice(half * KEYS, (half + 1) * KEYS)
        both = dot(ones, sb[0, 0, half], NT) + dot(ones, sb[0, 1, half], NT)
        db[0, :, lanes] = both[0:1, :]

    for p in range(2):
        q_copy(3, p).start()
        q_copy(1, 1 - p).start()
    for k in (1, 3, 2):
        d_copy(k).start()

    key_wide = kr_ref[...].astype(f32)
    key_inv = lax.rsqrt(jnp.mean(key_wide * key_wide, axis=1, keepdims=True) + EPS)
    own_keys = (key_wide * key_inv * kg_ref[...]).astype(bf16)
    slot_j = lax.broadcasted_iota(jnp.int32, (CAP, ROWS), 0)
    slot_i = lax.broadcasted_iota(jnp.int32, (CAP, ROWS), 1) & (CAP - 1)
    slot_j, slot_i = slot_j.astype(f32), slot_i.astype(f32)
    seg_j = jnp.where(slot_j >= len1, 1.0, 0.0)
    seg_i = jnp.where(slot_i >= len1, 1.0, 0.0)
    allowed = (slot_j <= slot_i) & (slot_i < total) & (seg_j == seg_i)
    e = jnp.where(allowed, jnp.exp2(dot(own_keys, qb[0, 0], NT)), 0.0)
    g = e * (dot(rv_ref[...], qb[0, 1], NT) - db[0])
    rs[0] = jnp.sum(e.reshape(CAP // 8, 8, ROWS), axis=0)
    for i in range(1, 4):
        rs[i] = jnp.zeros((8, ROWS), f32)
    se[...] = e.astype(bf16)
    sg[...] = g.astype(bf16)
    dqs[...] = dot(own_keys, sg[...], TN)

    def block(keys, values, i):
        n = keys.shape[0]
        e = jnp.exp2(dot(keys, qb[i, 0], NT))
        rs[i] += jnp.sum(e.reshape(n // 8, 8, ROWS), axis=0)
        g = e * (dot(values, qb[i, 1], NT) - db[i])
        return e.astype(bf16), g.astype(bf16)

    q_copy(3, 0).wait_recv()
    q_copy(2, 0).start()
    q_copy(1, 1).wait_recv()
    q_copy(2, 1).start()
    kt[0, :, 0:KEYS] = kb[0, 0].T
    for j in (1, 3, 2):
        k_copy(j, 0).wait_recv()
        kt[0, :, j * KEYS : (j + 1) * KEYS] = kb[j, 0].T
    for j in (1, 3, 2):
        k_copy(j, 1).wait_recv()

    def pass_on(p):
        k_copy(4, p).wait_recv()
        for j in (5, 7, 6):
            k_copy(j, p).start()

    pass_on(0)

    def near(m, carry):
        i = jnp.where(m == 2, 3, jnp.where(m == 3, 2, m))

        @pl.when(m == 1)
        def _():
            pass_on(1)
            q_copy(1, 0).wait_recv()
            d_copy(1).wait_recv()

        @pl.when(m == 2)
        def _():
            q_copy(3, 1).wait_recv()
            d_copy(3).wait_recv()

        @pl.when(m == 3)
        def _():
            q_copy(2, 0).wait_recv()
            q_copy(2, 1).wait_recv()
            d_copy(2).wait_recv()

        e, g = block(
            kb[0:4, 0].reshape(4 * KEYS, HD), kb[0:4, 1].reshape(4 * KEYS, HD), i
        )
        eg[0, 0:4, i] = e.reshape(4, KEYS, ROWS)
        eg[1, 0:4, i] = g.reshape(4, KEYS, ROWS)
        dqt[i] = dot(kt[0], g, NN)
        return carry

    lax.fori_loop(0, 4, near, 0)

    def far(m, carry):
        j = jnp.where(m == 2, 7, jnp.where(m == 3, 6, m + 4))

        for jj, step in ((5, 1), (7, 2), (6, 3)):

            @pl.when(m == step)
            def _():
                k_copy(jj, 0).wait_recv()
                k_copy(jj, 1).wait_recv()

        keys, values = kb[j, 0], kb[j, 1]
        for i in range(4):
            e, g = block(keys, values, i)
            eg[0, j, i] = e
            eg[1, j, i] = g
        return carry

    lax.fori_loop(0, 4, far, 0)

    for i in range(4):
        rss[i] = jnp.sum(rs[i], axis=0, keepdims=True)
    for k in (2, 1, 3):
        n_copy(k).start()

    for j in range(4):
        kt[1, :, j * KEYS : (j + 1) * KEYS] = kb[4 + j, 0].T

    def rest(m, carry):
        i = jnp.where(m == 2, 1, m + 2)
        dqt[i] += dot(kt[1], eg[1, 4:8, i].reshape(4 * KEYS, ROWS), NN)
        dqsend[i] = dqt[i].astype(bf16)

        for k in (1, 2, 3):

            @pl.when(i == 4 - k)
            def _():
                g_copy(k).start()

        return carry

    lax.fori_loop(0, 3, rest, 0)
    for k in (1, 3, 2):
        n_copy(k).wait_recv()
    for i in range(4):
        norm = rss[i]
        for k in (1, 2, 3):
            norm = norm + rsr[k, (i + 4 - k) % 4]
        inv = 1.0 / norm
        if i == 0:
            invr[...] = inv
        for c in range(4):
            part = slice(c * HD, (c + 1) * HD)
            column = jnp.broadcast_to(inv[:, part], (HD, HD)).T
            qn[0, i, part, :] = (qb[i, 1, part, :].astype(f32) * column).astype(bf16)
            column = column * math.log(2.0)
            qn[1, i, part, :] = (qb[i, 0, part, :].astype(f32) * column).astype(bf16)

    def plane_sum(plane, t):
        for s in (1, 3, 2):
            r_copy(plane, t, 4 - s).wait_recv()
        total = acc[plane, t]
        for s in (1, 2, 3):
            total = total + rr[plane, t, s].astype(f32)
        return total

    def to_plane(t):
        zs[t] = plane_sum(1, t).astype(bf16)
        z_copy(t).start()

    def own_terms():
        last = dot(kt[1], eg[1, 4:8, 0].reshape(4 * KEYS, ROWS), NN)
        dqt[0] = dqt[0] + dqs[...] + last
        dqsend[0] = dqt[0].astype(bf16)
        ov_ref[...] = dot(se[...], qn[0, 0], NN).astype(bf16)
        kng = dot(sg[...], qn[1, 0], NN)
        wide = kr_ref[...].astype(f32)
        inv = lax.rsqrt(jnp.mean(wide * wide, axis=1, keepdims=True) + EPS)
        w = kng * kg_ref[...]
        mean = jnp.mean(w * wide, axis=1, keepdims=True)
        ok_ref[...] = (inv * w - wide * (inv * inv * inv * mean)).astype(bf16)
        stores[1].start()
        stores[2].start()
        key_gain = jnp.sum(kng * wide * inv, axis=0, keepdims=True)
        square = dot(dqsend[0], qn[1, 0], NN)
        for i in range(1, 4):
            square = square + dot(dqsend[i], qn[1, i], NN)
        one = lax.broadcasted_iota(jnp.int32, (HD, HD), 0)
        two = lax.broadcasted_iota(jnp.int32, (HD, HD), 1)
        query_gain = jnp.sum(jnp.where(one == two, square, 0.0), axis=0, keepdims=True) / gain
        both = jnp.concatenate([query_gain, key_gain, jnp.zeros((6, HD), f32)], axis=0)
        gsrc[0] = both
        gz[z] = both
        for k in (4, 3, 5, 2, 6, 1, 7):
            gz_copy(k).start()

    def gains_y():
        for k in range(1, 8):
            gz_copy(k).wait_recv()
        both = gz[0]
        for k in range(1, 8):
            both = both + gz[k]
        gsrc[1] = both
        gy[y] = both
        for k in (2, 1, 3):
            gy_copy(k).start()

    def gains_x():
        for k in (1, 3, 2):
            gy_copy(k).wait_recv()
        both = gy[0] + gy[1] + gy[2] + gy[3]
        gsrc[2] = both
        stores[5].start()
        for k in (4, 5, 2, 3, 6, 7, 1):
            gx_copy(k).start()

    def terms(n, carry):
        plane = 1 - n // 8
        t = (n // 4) % 2
        m = n % 4
        kk = jnp.where(m == 0, 2, jnp.where(m == 2, 3, jnp.where(m == 3, 0, 1)))

        @pl.when(n == 2)
        def _():
            own_terms()

        @pl.when(n == 12)
        def _():
            to_plane(0)

        @pl.when(n == 14)
        def _():
            gains_y()
            for k in (1, 3, 2):
                r_copy(0, 0, k).start()

        j = plane * 4 + kk
        part = dot(eg[t, j, 0], qn[t, 0], NN)
        for i in range(1, 4):
            part = part + dot(eg[t, j, i], qn[t, i], NN)
        sb[plane, t, kk] = part.astype(bf16)

        @pl.when((m < 3) & (n < 8))
        def _():
            r_copy(1, t, kk).start()

        @pl.when(m == 3)
        def _():
            acc[plane, t] = part

        return carry

    lax.fori_loop(0, 16, terms, 0)
    to_plane(1)
    for k in (1, 3, 2):
        r_copy(0, 1, k).start()

    for k in (1, 3, 2):
        g_copy(k).wait_recv()
    for c in range(4):
        part = slice(c * HD, (c + 1) * HD)
        turned = dqt[0, :, part]
        for k in (1, 2, 3):
            turned = turned + dqr[k, :, part].astype(f32)
        grad = (turned * (invr[:, part] * scale)).T
        for h in (2 * c, 2 * c + 1):
            wide, inv = q_head(h)
            u = grad[(h % 2) * CAP : (h % 2 + 1) * CAP, :] * gain
            mean = jnp.mean(u * wide, axis=1, keepdims=True)
            found = inv * u - wide * (inv * inv * inv * mean)
            oq_ref[:, h * HD : (h + 1) * HD] = found.astype(bf16)
    stores[0].start()

    gains_x()
    opv_ref[...] = plane_sum(0, 0)
    stores[4].start()
    opk_ref[...] = plane_sum(0, 1)
    stores[3].start()
    for k in range(1, 8):
        gx_copy(k).wait_recv()
    for t in range(2):
        z_copy(t).wait_recv()

    for p in range(2):
        for j in range(1, 8):
            k_copy(j, p).wait_send()
        for k in (1, 2, 3):
            q_copy(k, p).wait_send()
    for k in (1, 2, 3):
        for make in (d_copy, n_copy, g_copy, gy_copy):
            make(k).wait_send()
        for plane in range(2):
            for t in range(2):
                r_copy(plane, t, k).wait_send()
    for t in range(2):
        z_copy(t).wait_send()
    for k in range(1, 8):
        gz_copy(k).wait_send()
        gx_copy(k).wait_send()
    for one in stores:
        one.wait()


def deliver(*refs):
    ins, outs, held, ends, into, out = (
        refs[:7], refs[7:14], refs[14:21], refs[21:23], refs[23], refs[24],
    )
    first = [pltpu.make_async_copy(ins[i], held[i], into.at[i]) for i in range(7)]
    then = [
        pltpu.make_async_copy(src, outs[i], out.at[i])
        for i, src in enumerate((*held[:5], *ends))
    ]
    for one in first:
        one.start()
    for one in first:
        one.wait()
    held[3][...] += held[5][1].astype(f32)
    then[3].start()
    held[4][...] += held[5][0].astype(f32)
    for i in (4, 0, 1, 2):
        then[i].start()
    both = held[6][0]
    for k in range(1, 8):
        both = both + held[6][k]
    for i in range(2):
        ends[i][...] = both[i : i + 1, :]
        then[5 + i].start()
    for two in then:
        two.wait()


def shards(qr, kr, rv, ao, og, pk, pv, qg, kg, lengths, holders):
    shapes = (
        jax.ShapeDtypeStruct((CAP, HEADS * HD), bf16),
        jax.ShapeDtypeStruct((CAP, HD), bf16),
        jax.ShapeDtypeStruct((CAP, HD), bf16),
        jax.ShapeDtypeStruct((KEYS, HD), f32),
        jax.ShapeDtypeStruct((KEYS, HD), f32),
    )
    gains = (jax.ShapeDtypeStruct((1, HD), f32),) * 2
    arrived = (
        jax.ShapeDtypeStruct((2, KEYS, HD), bf16),
        jax.ShapeDtypeStruct((8, 8, HD), f32),
    )
    somewhere = pl.BlockSpec(memory_space=pl.ANY)
    outs = pl.pallas_call(
        kernel,
        name="attention_backward",
        out_shape=(*shapes, *arrived),
        in_specs=[somewhere] * 11,
        out_specs=(somewhere,) * 7,
        scratch_shapes=[
            pltpu.VMEM((CAP, HEADS * HD), bf16),
            pltpu.VMEM((CAP, HD), bf16),
            pltpu.VMEM((CAP, HD), bf16),
            pltpu.VMEM((KEYS, HD), f32),
            pltpu.VMEM((KEYS, HD), f32),
            pltpu.VMEM((CAP, HEADS * HD), bf16),
            pltpu.VMEM((CAP, HD), bf16),
            pltpu.VMEM((CAP, HD), bf16),
            pltpu.VMEM((CAP, HEADS * HD), bf16),
            pltpu.VMEM((CAP, HEADS * HD), bf16),
            pltpu.VMEM((1, HD), f32),
            pltpu.VMEM((1, HD), f32),
            pltpu.VMEM((1, 64), jnp.int32),
            pltpu.VMEM((1, 64), jnp.int32),
            pltpu.VMEM((4, 2, ROWS, HD), bf16),
            pltpu.VMEM((4, 1, ROWS), f32),
            pltpu.VMEM((8, 2, KEYS, HD), bf16),
            pltpu.VMEM((2, HD, 4 * KEYS), bf16),
            pltpu.VMEM((2, 8, 4, KEYS, ROWS), bf16),
            pltpu.VMEM((4, HD, ROWS), f32),
            pltpu.VMEM((4, 8, ROWS), f32),
            pltpu.VMEM((4, 1, ROWS), f32),
            pltpu.VMEM((4, 4, 1, ROWS), f32),
            pltpu.VMEM((2, 4, ROWS, HD), bf16),
            pltpu.VMEM((1, ROWS), f32),
            pltpu.VMEM((HD, ROWS), f32),
            pltpu.VMEM((4, HD, ROWS), bf16),
            pltpu.VMEM((4, HD, ROWS), bf16),
            pltpu.VMEM((CAP, ROWS), bf16),
            pltpu.VMEM((CAP, ROWS), bf16),
            pltpu.VMEM((2, 2, 4, KEYS, HD), bf16),
            pltpu.VMEM((2, 2, KEYS, HD), f32),
            pltpu.VMEM((2, 2, 4, KEYS, HD), bf16),
            pltpu.VMEM((2, KEYS, HD), bf16),
            pltpu.VMEM((4, 8, HD), f32),
            pltpu.VMEM((8, 8, HD), f32),
            pltpu.VMEM((3, 8, HD), f32),
            pltpu.SemaphoreType.DMA((N_SEM,)),
            pltpu.SemaphoreType.DMA((N_SEM,)),
            pltpu.SemaphoreType.DMA((11,)),
            pltpu.SemaphoreType.DMA((6,)),
        ],
        compiler_params=pltpu.CompilerParams(
            collective_id=0, has_side_effects=True, vmem_limit_bytes=60 << 20
        ),
    )(qr, kr, rv, ao, og, pk, pv, qg.reshape(1, HD), kg.reshape(1, HD), lengths, holders)
    outs = pl.pallas_call(
        deliver,
        name="deliver",
        out_shape=(*shapes, *gains),
        in_specs=[somewhere] * 7,
        out_specs=(somewhere,) * 7,
        scratch_shapes=[pltpu.VMEM(shape.shape, shape.dtype) for shape in (*shapes, *arrived, *gains)]
        + [pltpu.SemaphoreType.DMA((7,))] * 2,
        compiler_params=pltpu.CompilerParams(vmem_limit_bytes=60 << 20),
    )(*outs)
    return (*outs[:5], outs[5].reshape(HD), outs[6].reshape(HD))


def solution(mesh):
    rows = P(("grp", "dev"), None)
    return jax.shard_map(
        shards,
        mesh=mesh,
        in_specs=(rows,) * 7 + (P(), P(), P("grp", None), P("grp", None)),
        out_specs=(rows,) * 5 + (P(), P()),
        check_vma=False,
    )
```

```python
import functools
import math

import jax
import jax.numpy as jnp
from jax import lax
from jax.experimental import pallas as pl
from jax.experimental.pallas import tpu as pltpu
from jax.sharding import PartitionSpec as P

f32 = jnp.float32
bf16 = jnp.bfloat16
MESH = pl.DeviceIdType.MESH
EPS = 1e-06
HEADS = 8
HD = 128
CAP = 64
ROWS = HEADS * CAP
KEYS = 256
NT = (((1,), (1,)), ((), ()))
NN = (((1,), (0,)), ((), ()))
TN = (((0,), (0,)), ((), ()))
S_Q, S_D, S_K, S_N, S_G, S_R, S_Z, S_X, S_Y, S_V = 0, 8, 12, 28, 32, 36, 52, 54, 62, 66
N_SEM = 74


def dot(a, b, dims):
    return lax.dot_general(a, b, dims, preferred_element_type=f32)


def kernel(
    qr_in, kr_in, rv_in, ao_in, og_in, pk_in, pv_in, qg_in, kg_in, len_in, hold_in,
    oq_out, ok_out, ov_out, opk_out, opv_out, zr_out, gx_out,
    oq_ref, ok_ref, ov_ref, opk_ref, opv_ref,
    qr_ref, kr_ref, rv_ref, ao_ref, og_ref, qg_ref, kg_ref, len_ref, hold_ref,
    qb, db, kb, kt, eg, dqt, rs, rss, rsr, qn, invr, dqs, dqsend, dqr,
    se, sg, sb, acc, rr, zs, gy, gz, gsrc, send, recv, load, store,
):
    grp = lax.axis_index("grp")
    dev = lax.axis_index("dev")
    x, y, z = dev // 8, (dev // 2) % 4, (dev % 2) * 4 + grp // 2
    core = grp % 2
    scale = HD ** (-0.5)

    def at(x=x, y=y, z=z, core=core):
        return ((z % 4) * 2 + core, x * 8 + y * 2 + z // 4)

    def xk(k):
        return at(x=(x + 4 - k) % 4)

    def yk(k):
        return at(y=(y + 4 - k) % 4)

    def zk(k):
        return at(z=(z + 8 - k) % 8)

    def copy(src, dst, sem, to):
        return pltpu.make_async_remote_copy(
            src_ref=src, dst_ref=dst, send_sem=send.at[sem], recv_sem=recv.at[sem],
            device_id=to, device_id_type=MESH,
        )

    def q_copy(k, p):
        src = qb.at[0, p] if k != 2 else qb.at[3 - 2 * p, p]
        return copy(src, qb.at[k, p], S_Q + 2 * k + p, xk(k if k != 2 else 3 - 2 * p))

    def d_copy(k):
        return copy(db.at[0], db.at[k], S_D + k, xk(k))

    def k_copy(j, p):
        src = (pk_in, pv_in)[p] if j <= 4 else kb.at[4, p]
        return copy(src, kb.at[j, p], S_K + 2 * j + p, zk(4) if j == 4 else yk(j % 4))

    def n_copy(k):
        return copy(rss, rsr.at[k], S_N + k, xk(k))

    def g_copy(k):
        return copy(dqsend.at[4 - k], dqr.at[k], S_G + k, xk(k))

    def r_copy(plane, t, kk):
        s = (4 - kk) % 4
        return copy(
            sb.at[plane, t, kk], rr.at[plane, t, s], S_R + plane * 8 + t * 4 + s, yk(s)
        )

    def z_copy(t):
        return copy(zs.at[t], zr_out.at[t], S_Z + t, zk(4))

    def gx_to(k):
        return at(x=(x + 4 - k // 2) % 4, core=(core + k) % 2)

    def gz_copy(k):
        return copy(gsrc.at[0], gz.at[z], S_V + k, zk(k))

    def gy_copy(k):
        return copy(gsrc.at[1], gy.at[y], S_Y + k, yk(k))

    def gx_copy(k):
        return copy(gsrc.at[2], gx_out.at[x * 2 + core], S_X + k, gx_to(k))

    loads = [
        pltpu.make_async_copy(src, dst, load.at[n])
        for n, (src, dst) in enumerate(
            (
                (pk_in, kb.at[0, 0]), (pv_in, kb.at[0, 1]), (hold_in, hold_ref), (len_in, len_ref),
                (qg_in, qg_ref), (kg_in, kg_ref), (qr_in, qr_ref), (og_in, og_ref), (ao_in, ao_ref),
                (kr_in, kr_ref), (rv_in, rv_ref),
            )
        )
    ]
    for one in loads:
        one.start()

    stores = [
        pltpu.make_async_copy(src, dst, store.at[n])
        for n, (src, dst) in enumerate(
            (
                (oq_ref, oq_out), (ok_ref, ok_out), (ov_ref, ov_out), (opk_ref, opk_out),
                (opv_ref, opv_out), (gsrc.at[2], gx_out.at[x * 2 + core]),
            )
        )
    ]

    barrier = pltpu.get_barrier_semaphore()
    partners = [gx_to(k) for k in range(1, 8)] + [yk(k) for k in (1, 2, 3)]
    partners += [zk(k) for k in range(1, 8)]
    for to in partners:
        pl.semaphore_signal(barrier, inc=1, device_id=to, device_id_type=MESH)

    pl.semaphore_wait(barrier, len(partners))
    for p in range(2):
        k_copy(4, p).start()
    for p in range(2):
        for j in (1, 3, 2):
            k_copy(j, p).start()
    for one in loads:
        one.wait()
    held = hold_ref[...] == dev
    mine = jnp.where(held, len_ref[...].astype(f32), 0.0)
    place = lax.broadcasted_iota(jnp.int32, (1, 64), 1).astype(f32)
    total = jnp.sum(mine, axis=1, keepdims=True)
    first = jnp.min(jnp.where(held, place, 64.0), axis=1, keepdims=True)
    len1 = jnp.sum(jnp.where(place == first, mine, 0.0), axis=1, keepdims=True)
    live = lax.broadcasted_iota(jnp.int32, (CAP, HD), 0).astype(f32) < total
    gain = qg_ref[...]

    def q_head(h):
        wide = qr_ref[:, h * HD : (h + 1) * HD].astype(f32)
        inv = lax.rsqrt(jnp.mean(wide * wide, axis=1, keepdims=True) + EPS)
        return wide, inv

    ones = jnp.ones((8, HD), bf16)
    for h in range(HEADS):
        cols = slice(h * HD, (h + 1) * HD)
        rows = slice(h * CAP, (h + 1) * CAP)
        wide, inv = q_head(h)
        normed = wide * inv * (gain * (scale * math.log2(math.e)))
        qb[0, 0, rows, :] = jnp.where(live, normed, 0.0).astype(bf16)
        grad = jnp.where(live, og_ref[:, cols].astype(f32), 0.0)
        qb[0, 1, rows, :] = grad.astype(bf16)
        prod = grad * ao_ref[:, cols].astype(f32)
        high = prod.astype(bf16)
        low = (prod - high.astype(f32)).astype(bf16)
        sb[0, 0, h // 4, (h % 4) * CAP : (h % 4 + 1) * CAP, :] = high
        sb[0, 1, h // 4, (h % 4) * CAP : (h % 4 + 1) * CAP, :] = low
    for half in range(2):
        lanes = slice(half * KEYS, (half + 1) * KEYS)
        both = dot(ones, sb[0, 0, half], NT) + dot(ones, sb[0, 1, half], NT)
        db[0, :, lanes] = both[0:1, :]

    for p in range(2):
        q_copy(3, p).start()
        q_copy(1, 1 - p).start()
    for k in (1, 3, 2):
        d_copy(k).start()

    key_wide = kr_ref[...].astype(f32)
    key_inv = lax.rsqrt(jnp.mean(key_wide * key_wide, axis=1, keepdims=True) + EPS)
    own_keys = (key_wide * key_inv * kg_ref[...]).astype(bf16)
    slot_j = lax.broadcasted_iota(jnp.int32, (CAP, ROWS), 0)
    slot_i = lax.broadcasted_iota(jnp.int32, (CAP, ROWS), 1) & (CAP - 1)
    slot_j, slot_i = slot_j.astype(f32), slot_i.astype(f32)
    seg_j = jnp.where(slot_j >= len1, 1.0, 0.0)
    seg_i = jnp.where(slot_i >= len1, 1.0, 0.0)
    allowed = (slot_j <= slot_i) & (slot_i < total) & (seg_j == seg_i)
    e = jnp.where(allowed, jnp.exp2(dot(own_keys, qb[0, 0], NT)), 0.0)
    g = e * (dot(rv_ref[...], qb[0, 1], NT) - db[0])
    rs[0] = jnp.sum(e.reshape(CAP // 8, 8, ROWS), axis=0)
    for i in range(1, 4):
        rs[i] = jnp.zeros((8, ROWS), f32)
    se[...] = e.astype(bf16)
    sg[...] = g.astype(bf16)
    dqs[...] = dot(own_keys, sg[...], TN)

    def block(keys, values, i):
        n = keys.shape[0]
        e = jnp.exp2(dot(keys, qb[i, 0], NT))
        rs[i] += jnp.sum(e.reshape(n // 8, 8, ROWS), axis=0)
        g = e * (dot(values, qb[i, 1], NT) - db[i])
        return e.astype(bf16), g.astype(bf16)

    q_copy(3, 0).wait_recv()
    q_copy(2, 0).start()
    q_copy(1, 1).wait_recv()
    q_copy(2, 1).start()
    kt[0, :, 0:KEYS] = kb[0, 0].T
    for j in (1, 3, 2):
        k_copy(j, 0).wait_recv()
        kt[0, :, j * KEYS : (j + 1) * KEYS] = kb[j, 0].T
    for j in (1, 3, 2):
        k_copy(j, 1).wait_recv()

    def pass_on(p):
        k_copy(4, p).wait_recv()
        for j in (5, 7, 6):
            k_copy(j, p).start()

    pass_on(0)

    def near(m, carry):
        i = jnp.where(m == 2, 3, jnp.where(m == 3, 2, m))

        @pl.when(m == 1)
        def _():
            pass_on(1)
            q_copy(1, 0).wait_recv()
            d_copy(1).wait_recv()

        @pl.when(m == 2)
        def _():
            q_copy(3, 1).wait_recv()
            d_copy(3).wait_recv()

        @pl.when(m == 3)
        def _():
            q_copy(2, 0).wait_recv()
            q_copy(2, 1).wait_recv()
            d_copy(2).wait_recv()

        e, g = block(
            kb[0:4, 0].reshape(4 * KEYS, HD), kb[0:4, 1].reshape(4 * KEYS, HD), i
        )
        eg[0, 0:4, i] = e.reshape(4, KEYS, ROWS)
        eg[1, 0:4, i] = g.reshape(4, KEYS, ROWS)
        dqt[i] = dot(kt[0], g, NN)
        return carry

    lax.fori_loop(0, 4, near, 0)

    def far(m, carry):
        j = jnp.where(m == 2, 7, jnp.where(m == 3, 6, m + 4))

        for jj, step in ((5, 1), (7, 2), (6, 3)):

            @pl.when(m == step)
            def _():
                k_copy(jj, 0).wait_recv()
                k_copy(jj, 1).wait_recv()

        keys, values = kb[j, 0], kb[j, 1]
        for i in range(4):
            e, g = block(keys, values, i)
            eg[0, j, i] = e
            eg[1, j, i] = g
        return carry

    lax.fori_loop(0, 4, far, 0)

    for i in range(4):
        rss[i] = jnp.sum(rs[i], axis=0, keepdims=True)
    for k in (2, 1, 3):
        n_copy(k).start()

    for j in range(4):
        kt[1, :, j * KEYS : (j + 1) * KEYS] = kb[4 + j, 0].T

    def rest(m, carry):
        i = jnp.where(m == 2, 1, m + 2)
        dqt[i] += dot(kt[1], eg[1, 4:8, i].reshape(4 * KEYS, ROWS), NN)
        dqsend[i] = dqt[i].astype(bf16)

        for k in (1, 2, 3):

            @pl.when(i == 4 - k)
            def _():
                g_copy(k).start()

        return carry

    lax.fori_loop(0, 3, rest, 0)
    for k in (1, 3, 2):
        n_copy(k).wait_recv()
    for i in range(4):
        norm = rss[i]
        for k in (1, 2, 3):
            norm = norm + rsr[k, (i + 4 - k) % 4]
        inv = 1.0 / norm
        if i == 0:
            invr[...] = inv
        for c in range(4):
            part = slice(c * HD, (c + 1) * HD)
            column = jnp.broadcast_to(inv[:, part], (HD, HD)).T
            qn[0, i, part, :] = (qb[i, 1, part, :].astype(f32) * column).astype(bf16)
            column = column * math.log(2.0)
            qn[1, i, part, :] = (qb[i, 0, part, :].astype(f32) * column).astype(bf16)

    def plane_sum(plane, t):
        for s in (1, 3, 2):
            r_copy(plane, t, 4 - s).wait_recv()
        total = acc[plane, t]
        for s in (1, 2, 3):
            total = total + rr[plane, t, s].astype(f32)
        return total

    def to_plane(t):
        zs[t] = plane_sum(1, t).astype(bf16)
        z_copy(t).start()

    def own_terms():
        last = dot(kt[1], eg[1, 4:8, 0].reshape(4 * KEYS, ROWS), NN)
        dqt[0] = dqt[0] + dqs[...] + last
        dqsend[0] = dqt[0].astype(bf16)
        ov_ref[...] = dot(se[...], qn[0, 0], NN).astype(bf16)
        kng = dot(sg[...], qn[1, 0], NN)
        wide = kr_ref[...].astype(f32)
        inv = lax.rsqrt(jnp.mean(wide * wide, axis=1, keepdims=True) + EPS)
        w = kng * kg_ref[...]
        mean = jnp.mean(w * wide, axis=1, keepdims=True)
        ok_ref[...] = (inv * w - wide * (inv * inv * inv * mean)).astype(bf16)
        stores[1].start()
        stores[2].start()
        key_gain = jnp.sum(kng * wide * inv, axis=0, keepdims=True)
        square = dot(dqsend[0], qn[1, 0], NN)
        for i in range(1, 4):
            square = square + dot(dqsend[i], qn[1, i], NN)
        one = lax.broadcasted_iota(jnp.int32, (HD, HD), 0)
        two = lax.broadcasted_iota(jnp.int32, (HD, HD), 1)
        query_gain = jnp.sum(jnp.where(one == two, square, 0.0), axis=0, keepdims=True) / gain
        both = jnp.concatenate([query_gain, key_gain, jnp.zeros((6, HD), f32)], axis=0)
        gsrc[0] = both
        gz[z] = both
        for k in (4, 3, 5, 2, 6, 1, 7):
            gz_copy(k).start()

    def gains_y():
        for k in range(1, 8):
            gz_copy(k).wait_recv()
        both = gz[0]
        for k in range(1, 8):
            both = both + gz[k]
        gsrc[1] = both
        gy[y] = both
        for k in (2, 1, 3):
            gy_copy(k).start()

    def gains_x():
        for k in (1, 3, 2):
            gy_copy(k).wait_recv()
        both = gy[0] + gy[1] + gy[2] + gy[3]
        gsrc[2] = both
        stores[5].start()
        for k in (4, 5, 2, 3, 6, 7, 1):
            gx_copy(k).start()

    def terms(n, carry):
        plane = 1 - n // 8
        t = (n // 4) % 2
        m = n % 4
        kk = jnp.where(m == 0, 2, jnp.where(m == 2, 3, jnp.where(m == 3, 0, 1)))

        @pl.when(n == 2)
        def _():
            own_terms()

        @pl.when(n == 12)
        def _():
            to_plane(0)

        @pl.when(n == 12)
        def _():
            gains_y()
            for k in (1, 3, 2):
                r_copy(0, 0, k).start()

        j = plane * 4 + kk
        part = dot(eg[t, j, 0], qn[t, 0], NN)
        for i in range(1, 4):
            part = part + dot(eg[t, j, i], qn[t, i], NN)
        sb[plane, t, kk] = part.astype(bf16)

        @pl.when((m < 3) & (n < 8))
        def _():
            r_copy(1, t, kk).start()

        @pl.when(m == 3)
        def _():
            acc[plane, t] = part

        return carry

    lax.fori_loop(0, 16, terms, 0)
    to_plane(1)
    for k in (1, 3, 2):
        r_copy(0, 1, k).start()

    for k in (1, 3, 2):
        g_copy(k).wait_recv()
    for c in range(4):
        part = slice(c * HD, (c + 1) * HD)
        turned = dqt[0, :, part]
        for k in (1, 2, 3):
            turned = turned + dqr[k, :, part].astype(f32)
        grad = (turned * (invr[:, part] * scale)).T
        for h in (2 * c, 2 * c + 1):
            wide, inv = q_head(h)
            u = grad[(h % 2) * CAP : (h % 2 + 1) * CAP, :] * gain
            mean = jnp.mean(u * wide, axis=1, keepdims=True)
            found = inv * u - wide * (inv * inv * inv * mean)
            oq_ref[:, h * HD : (h + 1) * HD] = found.astype(bf16)
    stores[0].start()

    gains_x()
    opv_ref[...] = plane_sum(0, 0)
    stores[4].start()
    opk_ref[...] = plane_sum(0, 1)
    stores[3].start()
    for k in range(1, 8):
        gx_copy(k).wait_recv()
    for t in range(2):
        z_copy(t).wait_recv()

    for p in range(2):
        for j in range(1, 8):
            k_copy(j, p).wait_send()
        for k in (1, 2, 3):
            q_copy(k, p).wait_send()
    for k in (1, 2, 3):
        for make in (d_copy, n_copy, g_copy, gy_copy):
            make(k).wait_send()
        for plane in range(2):
            for t in range(2):
                r_copy(plane, t, k).wait_send()
    for t in range(2):
        z_copy(t).wait_send()
    for k in range(1, 8):
        gz_copy(k).wait_send()
        gx_copy(k).wait_send()
    for one in stores:
        one.wait()


def deliver(*refs):
    ins, outs, held, ends, into, out = (
        refs[:7], refs[7:14], refs[14:21], refs[21:23], refs[23], refs[24],
    )
    first = [pltpu.make_async_copy(ins[i], held[i], into.at[i]) for i in range(7)]
    then = [
        pltpu.make_async_copy(src, outs[i], out.at[i])
        for i, src in enumerate((*held[:5], *ends))
    ]
    for one in first:
        one.start()
    for one in first:
        one.wait()
    held[3][...] += held[5][1].astype(f32)
    then[3].start()
    held[4][...] += held[5][0].astype(f32)
    for i in (4, 0, 1, 2):
        then[i].start()
    both = held[6][0]
    for k in range(1, 8):
        both = both + held[6][k]
    for i in range(2):
        ends[i][...] = both[i : i + 1, :]
        then[5 + i].start()
    for two in then:
        two.wait()


def shards(qr, kr, rv, ao, og, pk, pv, qg, kg, lengths, holders):
    shapes = (
        jax.ShapeDtypeStruct((CAP, HEADS * HD), bf16),
        jax.ShapeDtypeStruct((CAP, HD), bf16),
        jax.ShapeDtypeStruct((CAP, HD), bf16),
        jax.ShapeDtypeStruct((KEYS, HD), f32),
        jax.ShapeDtypeStruct((KEYS, HD), f32),
    )
    gains = (jax.ShapeDtypeStruct((1, HD), f32),) * 2
    arrived = (
        jax.ShapeDtypeStruct((2, KEYS, HD), bf16),
        jax.ShapeDtypeStruct((8, 8, HD), f32),
    )
    somewhere = pl.BlockSpec(memory_space=pl.ANY)
    outs = pl.pallas_call(
        kernel,
        name="attention_backward",
        out_shape=(*shapes, *arrived),
        in_specs=[somewhere] * 11,
        out_specs=(somewhere,) * 7,
        scratch_shapes=[
            pltpu.VMEM((CAP, HEADS * HD), bf16),
            pltpu.VMEM((CAP, HD), bf16),
            pltpu.VMEM((CAP, HD), bf16),
            pltpu.VMEM((KEYS, HD), f32),
            pltpu.VMEM((KEYS, HD), f32),
            pltpu.VMEM((CAP, HEADS * HD), bf16),
            pltpu.VMEM((CAP, HD), bf16),
            pltpu.VMEM((CAP, HD), bf16),
            pltpu.VMEM((CAP, HEADS * HD), bf16),
            pltpu.VMEM((CAP, HEADS * HD), bf16),
            pltpu.VMEM((1, HD), f32),
            pltpu.VMEM((1, HD), f32),
            pltpu.VMEM((1, 64), jnp.int32),
            pltpu.VMEM((1, 64), jnp.int32),
            pltpu.VMEM((4, 2, ROWS, HD), bf16),
            pltpu.VMEM((4, 1, ROWS), f32),
            pltpu.VMEM((8, 2, KEYS, HD), bf16),
            pltpu.VMEM((2, HD, 4 * KEYS), bf16),
            pltpu.VMEM((2, 8, 4, KEYS, ROWS), bf16),
            pltpu.VMEM((4, HD, ROWS), f32),
            pltpu.VMEM((4, 8, ROWS), f32),
            pltpu.VMEM((4, 1, ROWS), f32),
            pltpu.VMEM((4, 4, 1, ROWS), f32),
            pltpu.VMEM((2, 4, ROWS, HD), bf16),
            pltpu.VMEM((1, ROWS), f32),
            pltpu.VMEM((HD, ROWS), f32),
            pltpu.VMEM((4, HD, ROWS), bf16),
            pltpu.VMEM((4, HD, ROWS), bf16),
            pltpu.VMEM((CAP, ROWS), bf16),
            pltpu.VMEM((CAP, ROWS), bf16),
            pltpu.VMEM((2, 2, 4, KEYS, HD), bf16),
            pltpu.VMEM((2, 2, KEYS, HD), f32),
            pltpu.VMEM((2, 2, 4, KEYS, HD), bf16),
            pltpu.VMEM((2, KEYS, HD), bf16),
            pltpu.VMEM((4, 8, HD), f32),
            pltpu.VMEM((8, 8, HD), f32),
            pltpu.VMEM((3, 8, HD), f32),
            pltpu.SemaphoreType.DMA((N_SEM,)),
            pltpu.SemaphoreType.DMA((N_SEM,)),
            pltpu.SemaphoreType.DMA((11,)),
            pltpu.SemaphoreType.DMA((6,)),
        ],
        compiler_params=pltpu.CompilerParams(
            collective_id=0, has_side_effects=True, vmem_limit_bytes=60 << 20
        ),
    )(qr, kr, rv, ao, og, pk, pv, qg.reshape(1, HD), kg.reshape(1, HD), lengths, holders)
    outs = pl.pallas_call(
        deliver,
        name="deliver",
        out_shape=(*shapes, *gains),
        in_specs=[somewhere] * 7,
        out_specs=(somewhere,) * 7,
        scratch_shapes=[pltpu.VMEM(shape.shape, shape.dtype) for shape in (*shapes, *arrived, *gains)]
        + [pltpu.SemaphoreType.DMA((7,))] * 2,
        compiler_params=pltpu.CompilerParams(vmem_limit_bytes=60 << 20),
    )(*outs)
    return (*outs[:5], outs[5].reshape(HD), outs[6].reshape(HD))


def solution(mesh):
    rows = P(("grp", "dev"), None)
    return jax.shard_map(
        shards,
        mesh=mesh,
        in_specs=(rows,) * 7 + (P(), P(), P("grp", None), P("grp", None)),
        out_specs=(rows,) * 5 + (P(), P()),
        check_vma=False,
    )
```

```python
import functools
import math

import jax
import jax.numpy as jnp
from jax import lax
from jax.experimental import pallas as pl
from jax.experimental.pallas import tpu as pltpu
from jax.sharding import PartitionSpec as P

f32 = jnp.float32
bf16 = jnp.bfloat16
MESH = pl.DeviceIdType.MESH
EPS = 1e-06
HEADS = 8
HD = 128
CAP = 64
ROWS = HEADS * CAP
KEYS = 256
NT = (((1,), (1,)), ((), ()))
NN = (((1,), (0,)), ((), ()))
TN = (((0,), (0,)), ((), ()))
S_Q, S_D, S_K, S_N, S_G, S_R, S_Z, S_X, S_Y, S_V = 0, 8, 12, 28, 32, 36, 52, 54, 62, 66
N_SEM = 74


def dot(a, b, dims):
    return lax.dot_general(a, b, dims, preferred_element_type=f32)


def kernel(
    qr_in, kr_in, rv_in, ao_in, og_in, pk_in, pv_in, qg_in, kg_in, len_in, hold_in,
    oq_out, ok_out, ov_out, opk_out, opv_out, zr_out, gx_out,
    oq_ref, ok_ref, ov_ref, opk_ref, opv_ref,
    qr_ref, kr_ref, rv_ref, ao_ref, og_ref, qg_ref, kg_ref, len_ref, hold_ref,
    qb, db, kb, kt, eg, dqt, rs, rss, rsr, qn, invr, dqs, dqsend, dqr,
    se, sg, sb, acc, rr, zs, gy, gz, gsrc, send, recv, load, store,
):
    grp = lax.axis_index("grp")
    dev = lax.axis_index("dev")
    x, y, z = dev // 8, (dev // 2) % 4, (dev % 2) * 4 + grp // 2
    core = grp % 2
    scale = HD ** (-0.5)

    def at(x=x, y=y, z=z, core=core):
        return ((z % 4) * 2 + core, x * 8 + y * 2 + z // 4)

    def xk(k):
        return at(x=(x + 4 - k) % 4)

    def yk(k):
        return at(y=(y + 4 - k) % 4)

    def zk(k):
        return at(z=(z + 8 - k) % 8)

    def copy(src, dst, sem, to):
        return pltpu.make_async_remote_copy(
            src_ref=src, dst_ref=dst, send_sem=send.at[sem], recv_sem=recv.at[sem],
            device_id=to, device_id_type=MESH,
        )

    def q_copy(k, p):
        src = qb.at[0, p] if k != 2 else qb.at[3 - 2 * p, p]
        return copy(src, qb.at[k, p], S_Q + 2 * k + p, xk(k if k != 2 else 3 - 2 * p))

    def d_copy(k):
        return copy(db.at[0], db.at[k], S_D + k, xk(k))

    def k_copy(j, p):
        src = (pk_in, pv_in)[p] if j <= 4 else kb.at[4, p]
        return copy(src, kb.at[j, p], S_K + 2 * j + p, zk(4) if j == 4 else yk(j % 4))

    def n_copy(k):
        return copy(rss, rsr.at[k], S_N + k, xk(k))

    def g_copy(k):
        return copy(dqsend.at[4 - k], dqr.at[k], S_G + k, xk(k))

    def r_copy(plane, t, kk):
        s = (4 - kk) % 4
        return copy(
            sb.at[plane, t, kk], rr.at[plane, t, s], S_R + plane * 8 + t * 4 + s, yk(s)
        )

    def z_copy(t):
        return copy(zs.at[t], zr_out.at[t], S_Z + t, zk(4))

    def gx_to(k):
        return at(x=(x + 4 - k // 2) % 4, core=(core + k) % 2)

    def gz_copy(k):
        return copy(gsrc.at[0], gz.at[z], S_V + k, zk(k))

    def gy_copy(k):
        return copy(gsrc.at[1], gy.at[y], S_Y + k, yk(k))

    def gx_copy(k):
        return copy(gsrc.at[2], gx_out.at[x * 2 + core], S_X + k, gx_to(k))

    loads = [
        pltpu.make_async_copy(src, dst, load.at[n])
        for n, (src, dst) in enumerate(
            (
                (pk_in, kb.at[0, 0]), (pv_in, kb.at[0, 1]), (hold_in, hold_ref), (len_in, len_ref),
                (qg_in, qg_ref), (kg_in, kg_ref), (qr_in, qr_ref), (og_in, og_ref), (ao_in, ao_ref),
                (kr_in, kr_ref), (rv_in, rv_ref),
            )
        )
    ]
    for one in loads:
        one.start()

    stores = [
        pltpu.make_async_copy(src, dst, store.at[n])
        for n, (src, dst) in enumerate(
            (
                (oq_ref, oq_out), (ok_ref, ok_out), (ov_ref, ov_out), (opk_ref, opk_out),
                (opv_ref, opv_out), (gsrc.at[2], gx_out.at[x * 2 + core]),
            )
        )
    ]

    barrier = pltpu.get_barrier_semaphore()
    partners = [gx_to(k) for k in range(1, 8)] + [yk(k) for k in (1, 2, 3)]
    partners += [zk(k) for k in range(1, 8)]
    for to in partners:
        pl.semaphore_signal(barrier, inc=1, device_id=to, device_id_type=MESH)

    pl.semaphore_wait(barrier, len(partners))
    for p in range(2):
        k_copy(4, p).start()
    for p in range(2):
        for j in (1, 3, 2):
            k_copy(j, p).start()
    for one in loads:
        one.wait()
    held = hold_ref[...] == dev
    mine = jnp.where(held, len_ref[...].astype(f32), 0.0)
    place = lax.broadcasted_iota(jnp.int32, (1, 64), 1).astype(f32)
    total = jnp.sum(mine, axis=1, keepdims=True)
    first = jnp.min(jnp.where(held, place, 64.0), axis=1, keepdims=True)
    len1 = jnp.sum(jnp.where(place == first, mine, 0.0), axis=1, keepdims=True)
    live = lax.broadcasted_iota(jnp.int32, (CAP, HD), 0).astype(f32) < total
    gain = qg_ref[...]

    def q_head(h):
        wide = qr_ref[:, h * HD : (h + 1) * HD].astype(f32)
        inv = lax.rsqrt(jnp.mean(wide * wide, axis=1, keepdims=True) + EPS)
        return wide, inv

    ones = jnp.ones((8, HD), bf16)
    for h in range(HEADS):
        cols = slice(h * HD, (h + 1) * HD)
        rows = slice(h * CAP, (h + 1) * CAP)
        wide, inv = q_head(h)
        normed = wide * inv * (gain * (scale * math.log2(math.e)))
        qb[0, 0, rows, :] = jnp.where(live, normed, 0.0).astype(bf16)
        grad = jnp.where(live, og_ref[:, cols].astype(f32), 0.0)
        qb[0, 1, rows, :] = grad.astype(bf16)
        prod = grad * ao_ref[:, cols].astype(f32)
        high = prod.astype(bf16)
        low = (prod - high.astype(f32)).astype(bf16)
        sb[0, 0, h // 4, (h % 4) * CAP : (h % 4 + 1) * CAP, :] = high
        sb[0, 1, h // 4, (h % 4) * CAP : (h % 4 + 1) * CAP, :] = low
    for half in range(2):
        lanes = slice(half * KEYS, (half + 1) * KEYS)
        both = dot(ones, sb[0, 0, half], NT) + dot(ones, sb[0, 1, half], NT)
        db[0, :, lanes] = both[0:1, :]

    for p in range(2):
        q_copy(3, p).start()
        q_copy(1, 1 - p).start()
    for k in (1, 3, 2):
        d_copy(k).start()

    key_wide = kr_ref[...].astype(f32)
    key_inv = lax.rsqrt(jnp.mean(key_wide * key_wide, axis=1, keepdims=True) + EPS)
    own_keys = (key_wide * key_inv * kg_ref[...]).astype(bf16)
    slot_j = lax.broadcasted_iota(jnp.int32, (CAP, ROWS), 0)
    slot_i = lax.broadcasted_iota(jnp.int32, (CAP, ROWS), 1) & (CAP - 1)
    slot_j, slot_i = slot_j.astype(f32), slot_i.astype(f32)
    seg_j = jnp.where(slot_j >= len1, 1.0, 0.0)
    seg_i = jnp.where(slot_i >= len1, 1.0, 0.0)
    allowed = (slot_j <= slot_i) & (slot_i < total) & (seg_j == seg_i)
    e = jnp.where(allowed, jnp.exp2(dot(own_keys, qb[0, 0], NT)), 0.0)
    g = e * (dot(rv_ref[...], qb[0, 1], NT) - db[0])
    rs[0] = jnp.sum(e.reshape(CAP // 8, 8, ROWS), axis=0)
    for i in range(1, 4):
        rs[i] = jnp.zeros((8, ROWS), f32)
    se[...] = e.astype(bf16)
    sg[...] = g.astype(bf16)
    dqs[...] = dot(own_keys, sg[...], TN)

    def block(keys, values, i):
        n = keys.shape[0]
        e = jnp.exp2(dot(keys, qb[i, 0], NT))
        rs[i] += jnp.sum(e.reshape(n // 8, 8, ROWS), axis=0)
        g = e * (dot(values, qb[i, 1], NT) - db[i])
        return e.astype(bf16), g.astype(bf16)

    def pass_on(p):
        k_copy(4, p).wait_recv()
        for j in (5, 7, 6):
            k_copy(j, p).start()

    pass_on(0)
    q_copy(3, 0).wait_recv()
    q_copy(2, 0).start()
    q_copy(1, 1).wait_recv()
    q_copy(2, 1).start()
    kt[0, :, 0:KEYS] = kb[0, 0].T
    for j in (1, 3, 2):
        k_copy(j, 0).wait_recv()
        kt[0, :, j * KEYS : (j + 1) * KEYS] = kb[j, 0].T
    for j in (1, 3, 2):
        k_copy(j, 1).wait_recv()

    pass_on(1)

    def near(m, carry):
        i = jnp.where(m == 2, 3, jnp.where(m == 3, 2, m))

        @pl.when(m == 1)
        def _():
            q_copy(1, 0).wait_recv()
            d_copy(1).wait_recv()

        @pl.when(m == 2)
        def _():
            q_copy(3, 1).wait_recv()
            d_copy(3).wait_recv()

        @pl.when(m == 3)
        def _():
            q_copy(2, 0).wait_recv()
            q_copy(2, 1).wait_recv()
            d_copy(2).wait_recv()

        e, g = block(
            kb[0:4, 0].reshape(4 * KEYS, HD), kb[0:4, 1].reshape(4 * KEYS, HD), i
        )
        eg[0, 0:4, i] = e.reshape(4, KEYS, ROWS)
        eg[1, 0:4, i] = g.reshape(4, KEYS, ROWS)
        dqt[i] = dot(kt[0], g, NN)
        return carry

    lax.fori_loop(0, 4, near, 0)

    def far(m, carry):
        j = jnp.where(m == 2, 7, jnp.where(m == 3, 6, m + 4))

        for jj, step in ((5, 1), (7, 2), (6, 3)):

            @pl.when(m == step)
            def _():
                k_copy(jj, 0).wait_recv()
                k_copy(jj, 1).wait_recv()

        keys, values = kb[j, 0], kb[j, 1]
        for i in range(4):
            e, g = block(keys, values, i)
            eg[0, j, i] = e
            eg[1, j, i] = g
        return carry

    lax.fori_loop(0, 4, far, 0)

    for i in range(4):
        rss[i] = jnp.sum(rs[i], axis=0, keepdims=True)
    for k in (2, 1, 3):
        n_copy(k).start()

    for j in range(4):
        kt[1, :, j * KEYS : (j + 1) * KEYS] = kb[4 + j, 0].T

    def rest(m, carry):
        i = jnp.where(m == 2, 1, m + 2)
        dqt[i] += dot(kt[1], eg[1, 4:8, i].reshape(4 * KEYS, ROWS), NN)
        dqsend[i] = dqt[i].astype(bf16)

        for k in (1, 2, 3):

            @pl.when(i == 4 - k)
            def _():
                g_copy(k).start()

        return carry

    lax.fori_loop(0, 3, rest, 0)
    for k in (1, 3, 2):
        n_copy(k).wait_recv()
    for i in range(4):
        norm = rss[i]
        for k in (1, 2, 3):
            norm = norm + rsr[k, (i + 4 - k) % 4]
        inv = 1.0 / norm
        if i == 0:
            invr[...] = inv
        for c in range(4):
            part = slice(c * HD, (c + 1) * HD)
            column = jnp.broadcast_to(inv[:, part], (HD, HD)).T
            qn[0, i, part, :] = (qb[i, 1, part, :].astype(f32) * column).astype(bf16)
            column = column * math.log(2.0)
            qn[1, i, part, :] = (qb[i, 0, part, :].astype(f32) * column).astype(bf16)

    def plane_sum(plane, t):
        for s in (1, 3, 2):
            r_copy(plane, t, 4 - s).wait_recv()
        total = acc[plane, t]
        for s in (1, 2, 3):
            total = total + rr[plane, t, s].astype(f32)
        return total

    def to_plane(t):
        zs[t] = plane_sum(1, t).astype(bf16)
        z_copy(t).start()

    def own_terms():
        last = dot(kt[1], eg[1, 4:8, 0].reshape(4 * KEYS, ROWS), NN)
        dqt[0] = dqt[0] + dqs[...] + last
        dqsend[0] = dqt[0].astype(bf16)
        ov_ref[...] = dot(se[...], qn[0, 0], NN).astype(bf16)
        kng = dot(sg[...], qn[1, 0], NN)
        wide = kr_ref[...].astype(f32)
        inv = lax.rsqrt(jnp.mean(wide * wide, axis=1, keepdims=True) + EPS)
        w = kng * kg_ref[...]
        mean = jnp.mean(w * wide, axis=1, keepdims=True)
        ok_ref[...] = (inv * w - wide * (inv * inv * inv * mean)).astype(bf16)
        stores[1].start()
        stores[2].start()
        key_gain = jnp.sum(kng * wide * inv, axis=0, keepdims=True)
        square = dot(dqsend[0], qn[1, 0], NN)
        for i in range(1, 4):
            square = square + dot(dqsend[i], qn[1, i], NN)
        one = lax.broadcasted_iota(jnp.int32, (HD, HD), 0)
        two = lax.broadcasted_iota(jnp.int32, (HD, HD), 1)
        query_gain = jnp.sum(jnp.where(one == two, square, 0.0), axis=0, keepdims=True) / gain
        both = jnp.concatenate([query_gain, key_gain, jnp.zeros((6, HD), f32)], axis=0)
        gsrc[0] = both
        gz[z] = both
        for k in (4, 3, 5, 2, 6, 1, 7):
            gz_copy(k).start()

    def gains_y():
        for k in range(1, 8):
            gz_copy(k).wait_recv()
        both = gz[0]
        for k in range(1, 8):
            both = both + gz[k]
        gsrc[1] = both
        gy[y] = both
        for k in (2, 1, 3):
            gy_copy(k).start()

    def gains_x():
        for k in (1, 3, 2):
            gy_copy(k).wait_recv()
        both = gy[0] + gy[1] + gy[2] + gy[3]
        gsrc[2] = both
        stores[5].start()
        for k in (4, 5, 2, 3, 6, 7, 1):
            gx_copy(k).start()

    def terms(n, carry):
        plane = 1 - n // 8
        t = (n // 4) % 2
        m = n % 4
        kk = jnp.where(m == 0, 2, jnp.where(m == 2, 3, jnp.where(m == 3, 0, 1)))

        @pl.when(n == 1)
        def _():
            own_terms()

        @pl.when(n == 12)
        def _():
            to_plane(0)

        @pl.when(n == 12)
        def _():
            gains_y()
            for k in (1, 3, 2):
                r_copy(0, 0, k).start()

        j = plane * 4 + kk
        part = dot(eg[t, j, 0], qn[t, 0], NN)
        for i in range(1, 4):
            part = part + dot(eg[t, j, i], qn[t, i], NN)
        sb[plane, t, kk] = part.astype(bf16)

        @pl.when((m < 3) & (n < 8))
        def _():
            r_copy(1, t, kk).start()

        @pl.when(m == 3)
        def _():
            acc[plane, t] = part

        return carry

    lax.fori_loop(0, 16, terms, 0)
    to_plane(1)
    for k in (1, 3, 2):
        r_copy(0, 1, k).start()

    gains_x()

    for k in (1, 3, 2):
        g_copy(k).wait_recv()
    for c in range(4):
        part = slice(c * HD, (c + 1) * HD)
        turned = dqt[0, :, part]
        for k in (1, 2, 3):
            turned = turned + dqr[k, :, part].astype(f32)
        grad = (turned * (invr[:, part] * scale)).T
        for h in (2 * c, 2 * c + 1):
            wide, inv = q_head(h)
            u = grad[(h % 2) * CAP : (h % 2 + 1) * CAP, :] * gain
            mean = jnp.mean(u * wide, axis=1, keepdims=True)
            found = inv * u - wide * (inv * inv * inv * mean)
            oq_ref[:, h * HD : (h + 1) * HD] = found.astype(bf16)
    stores[0].start()

    opv_ref[...] = plane_sum(0, 0)
    stores[4].start()
    opk_ref[...] = plane_sum(0, 1)
    stores[3].start()
    for k in range(1, 8):
        gx_copy(k).wait_recv()
    for t in range(2):
        z_copy(t).wait_recv()

    for p in range(2):
        for j in range(1, 8):
            k_copy(j, p).wait_send()
        for k in (1, 2, 3):
            q_copy(k, p).wait_send()
    for k in (1, 2, 3):
        for make in (d_copy, n_copy, g_copy, gy_copy):
            make(k).wait_send()
        for plane in range(2):
            for t in range(2):
                r_copy(plane, t, k).wait_send()
    for t in range(2):
        z_copy(t).wait_send()
    for k in range(1, 8):
        gz_copy(k).wait_send()
        gx_copy(k).wait_send()
    for one in stores:
        one.wait()


def deliver(*refs):
    ins, outs, held, ends, into, out = (
        refs[:7], refs[7:14], refs[14:21], refs[21:23], refs[23], refs[24],
    )
    first = [pltpu.make_async_copy(ins[i], held[i], into.at[i]) for i in range(7)]
    then = [
        pltpu.make_async_copy(src, outs[i], out.at[i])
        for i, src in enumerate((*held[:5], *ends))
    ]
    for one in first:
        one.start()
    for one in first:
        one.wait()
    held[3][...] += held[5][1].astype(f32)
    then[3].start()
    held[4][...] += held[5][0].astype(f32)
    for i in (4, 0, 1, 2):
        then[i].start()
    both = held[6][0]
    for k in range(1, 8):
        both = both + held[6][k]
    for i in range(2):
        ends[i][...] = both[i : i + 1, :]
        then[5 + i].start()
    for two in then:
        two.wait()


def shards(qr, kr, rv, ao, og, pk, pv, qg, kg, lengths, holders):
    shapes = (
        jax.ShapeDtypeStruct((CAP, HEADS * HD), bf16),
        jax.ShapeDtypeStruct((CAP, HD), bf16),
        jax.ShapeDtypeStruct((CAP, HD), bf16),
        jax.ShapeDtypeStruct((KEYS, HD), f32),
        jax.ShapeDtypeStruct((KEYS, HD), f32),
    )
    gains = (jax.ShapeDtypeStruct((1, HD), f32),) * 2
    arrived = (
        jax.ShapeDtypeStruct((2, KEYS, HD), bf16),
        jax.ShapeDtypeStruct((8, 8, HD), f32),
    )
    somewhere = pl.BlockSpec(memory_space=pl.ANY)
    outs = pl.pallas_call(
        kernel,
        name="attention_backward",
        out_shape=(*shapes, *arrived),
        in_specs=[somewhere] * 11,
        out_specs=(somewhere,) * 7,
        scratch_shapes=[
            pltpu.VMEM((CAP, HEADS * HD), bf16),
            pltpu.VMEM((CAP, HD), bf16),
            pltpu.VMEM((CAP, HD), bf16),
            pltpu.VMEM((KEYS, HD), f32),
            pltpu.VMEM((KEYS, HD), f32),
            pltpu.VMEM((CAP, HEADS * HD), bf16),
            pltpu.VMEM((CAP, HD), bf16),
            pltpu.VMEM((CAP, HD), bf16),
            pltpu.VMEM((CAP, HEADS * HD), bf16),
            pltpu.VMEM((CAP, HEADS * HD), bf16),
            pltpu.VMEM((1, HD), f32),
            pltpu.VMEM((1, HD), f32),
            pltpu.VMEM((1, 64), jnp.int32),
            pltpu.VMEM((1, 64), jnp.int32),
            pltpu.VMEM((4, 2, ROWS, HD), bf16),
            pltpu.VMEM((4, 1, ROWS), f32),
            pltpu.VMEM((8, 2, KEYS, HD), bf16),
            pltpu.VMEM((2, HD, 4 * KEYS), bf16),
            pltpu.VMEM((2, 8, 4, KEYS, ROWS), bf16),
            pltpu.VMEM((4, HD, ROWS), f32),
            pltpu.VMEM((4, 8, ROWS), f32),
            pltpu.VMEM((4, 1, ROWS), f32),
            pltpu.VMEM((4, 4, 1, ROWS), f32),
            pltpu.VMEM((2, 4, ROWS, HD), bf16),
            pltpu.VMEM((1, ROWS), f32),
            pltpu.VMEM((HD, ROWS), f32),
            pltpu.VMEM((4, HD, ROWS), bf16),
            pltpu.VMEM((4, HD, ROWS), bf16),
            pltpu.VMEM((CAP, ROWS), bf16),
            pltpu.VMEM((CAP, ROWS), bf16),
            pltpu.VMEM((2, 2, 4, KEYS, HD), bf16),
            pltpu.VMEM((2, 2, KEYS, HD), f32),
            pltpu.VMEM((2, 2, 4, KEYS, HD), bf16),
            pltpu.VMEM((2, KEYS, HD), bf16),
            pltpu.VMEM((4, 8, HD), f32),
            pltpu.VMEM((8, 8, HD), f32),
            pltpu.VMEM((3, 8, HD), f32),
            pltpu.SemaphoreType.DMA((N_SEM,)),
            pltpu.SemaphoreType.DMA((N_SEM,)),
            pltpu.SemaphoreType.DMA((11,)),
            pltpu.SemaphoreType.DMA((6,)),
        ],
        compiler_params=pltpu.CompilerParams(
            collective_id=0, has_side_effects=True, vmem_limit_bytes=60 << 20
        ),
    )(qr, kr, rv, ao, og, pk, pv, qg.reshape(1, HD), kg.reshape(1, HD), lengths, holders)
    outs = pl.pallas_call(
        deliver,
        name="deliver",
        out_shape=(*shapes, *gains),
        in_specs=[somewhere] * 7,
        out_specs=(somewhere,) * 7,
        scratch_shapes=[pltpu.VMEM(shape.shape, shape.dtype) for shape in (*shapes, *arrived, *gains)]
        + [pltpu.SemaphoreType.DMA((7,))] * 2,
        compiler_params=pltpu.CompilerParams(vmem_limit_bytes=60 << 20),
    )(*outs)
    return (*outs[:5], outs[5].reshape(HD), outs[6].reshape(HD))


def solution(mesh):
    rows = P(("grp", "dev"), None)
    return jax.shard_map(
        shards,
        mesh=mesh,
        in_specs=(rows,) * 7 + (P(), P(), P("grp", None), P("grp", None)),
        out_specs=(rows,) * 5 + (P(), P()),
        check_vma=False,
    )
```
